512 devices in a mesh: gx: 16 (over y, core), gy: 4 (over z_lo), gz: 8 (over x, z_hi).
Axes of the slice: x: 4, y: 8, z: 8 (z_hi: 2, z_lo: 4; z = z_hi * 4 + z_lo), core: 2. Of those that a mesh axis runs over, the one named last changes fastest.
Arguments:
- centre_coef: float32 [16384, 3], P(('gx', 'gy', 'gz')), may hold values from -6 to 6
- centre_index: int32 [16384], P(('gx', 'gy', 'gz')), may hold values from 0 to 65535, as said below
- stiff_factor: float32 [256, 256, 1024], P('gx', 'gy', 'gz'), may hold values from 0.5 to 4
- prev_disp: float32 [3, 256, 256, 1024], P(None, 'gx', 'gy', 'gz'), may hold values from -6 to 6
Outputs:
- displacement: float32 [3, 256, 256, 1024], P(None, 'gx', 'gy', 'gz')
The draws below stay inside these ranges and needn't reach their ends.
Inputs may be any that keep to these rules, and one draw needn't show every extreme that they name: `centre_index`: distinct wall nodes; the first and the last wall node are always among them.
All inputs are finite; a program needn't handle non-finite values.
Results may differ from the reference program's by a relative error of at most 0.0003.
Values sent between devices are 32-bit elements; how exact they have to be, the bound alone decides.
No kernel may reach another device: no remote copies, remote signals or barrier semaphores. Data moves between devices by JAX's collectives and lax.ppermute only.
A program may use at most 128 MiB of HBM per device.

```python
import math
import jax
import jax.numpy as jnp
from jax import lax

LZ = 1
NC = 16384
SWEEPS = 3
NX = 256
NY = 256
NZ = 1024


def draw_centre_index(key, part):
    key = jax.random.fold_in(key, 7)
    order_key, shuffle_key = jax.random.split(key)
    middle = jax.random.permutation(order_key, NX * NY - 2)[:NC - 2].astype(jnp.int32) + 1
    chosen = jnp.concatenate([jnp.array([0, NX * NY - 1], jnp.int32), middle])
    return jax.random.permutation(shuffle_key, chosen).astype(jnp.int32)


def block_levels(stream_key, dims, cuts, smallest, high):
    def one(dim, shards_of):
        draws = jax.random.uniform(jax.random.fold_in(jax.random.fold_in(stream_key, 6), dim), (shards_of,), jnp.float32, smallest / len(cuts), high / len(cuts))
        return jnp.repeat(jnp.exp(draws), dims[dim] // shards_of).reshape((-1,) + (1,) * (len(dims) - dim - 1))

    gain = one(*cuts[0])
    for cut in cuts[1:]:
        gain = gain * one(*cut)
    return gain


def gaussian(stream_key, shape, scale, reach, pieces=(), kind=jnp.bfloat16):
    entries = jax.random.normal(stream_key, shape, jnp.float32) * scale
    if len(pieces) > 0:
        entries = block_levels(stream_key, shape, pieces, -0.22, 0.18) * entries
    return jnp.clip(entries, min=-reach, max=reach).astype(kind)


def setup_inputs(seed: int = 0) -> dict:
    seeds = jax.random.split(jax.random.key(seed), 5)
    return {
        "centre_coef": gaussian(seeds[0], (NC, 3), 1.0, 6.0, ((0, 512),), jnp.float32),
        "centre_index": draw_centre_index(jax.random.fold_in(seeds[4], 71), 0),
        "stiff_factor": jnp.clip(jnp.exp(math.log(4.0) - 2.0794415 * jax.random.uniform(seeds[2], (NX, NY, NZ), jnp.float32) ** block_levels(seeds[2], (NX, NY, NZ), ((0, 16), (1, 4), (2, 8)), -0.2, 0.2)), 0.5, 4.0),
        "prev_disp": gaussian(seeds[3], (3, NX, NY, NZ), 1.0, 6.0, ((1, 16), (2, 4), (3, 8)), jnp.float32),
    }


RADIUS = 0.02
OMEGA = 0.8
NEIGHBOURS = ((1, 0, 0), (-1, 0, 0), (0, 1, 0), (0, -1, 0), (0, 0, 1), (0, 0, -1))

def interior(array, offset):
    ext_x, ext_y, ext_z = array.shape[-3:]
    return array[..., 1 + offset[0]:ext_x - 1 + offset[0], 1 + offset[1]:ext_y - 1 + offset[1], 1 + offset[2]:ext_z - 1 + offset[2]]

def relax_sweep(field_ext, stiff_ext, frozen, inside):
    centre_stiff = interior(stiff_ext, (0, 0, 0))
    current = interior(field_ext, (0, 0, 0))
    flux_total = jnp.zeros_like(current)
    diagonal = jnp.zeros_like(centre_stiff)
    for offset in NEIGHBOURS:
        face = 0.5 * (centre_stiff + interior(stiff_ext, offset))
        flux_total = flux_total + face * interior(field_ext, offset)
        diagonal = diagonal + face
    if inside is None:
        divisor = diagonal
    else:
        divisor = jnp.where(inside, diagonal, 1.0)
    updated = (1.0 - OMEGA) * current + OMEGA * (flux_total / divisor)
    updated = jnp.where(frozen, current, updated)
    if inside is not None:
        updated = jnp.where(inside, updated, 0.0)
    return updated

def wendland(dist_sq):
    ratio = jnp.sqrt(dist_sq) / RADIUS
    lead = jnp.maximum(1.0 - ratio, 0.0)
    return lead * lead * lead * lead * (4.0 * ratio + 1.0)

def kernel_sum(coef, index, node_x, node_y, node_z, count_x, count_y):
    centre_x = ((index // count_y).astype(jnp.float32) + 0.5) / count_x
    centre_y = ((index % count_y).astype(jnp.float32) + 0.5) / count_y
    dist_sq = (node_x[None, :] - centre_x[:, None]) ** 2 + (node_y[None, :] - centre_y[:, None]) ** 2 + (node_z ** 2)[None, :]
    weights = wendland(dist_sq)
    return jnp.dot(coef.T, weights, precision=lax.Precision.HIGHEST, preferred_element_type=jnp.float32)

def reference(centre_coef, centre_index, stiff_factor, prev_disp):
    rows_per = math.gcd(NX, 16)
    index_x = jnp.arange(NX, dtype=jnp.int32).astype(jnp.float32)
    index_y = jnp.arange(NY, dtype=jnp.int32).astype(jnp.float32)
    index_z = jnp.arange(LZ, dtype=jnp.int32).astype(jnp.float32)
    node_x = jnp.broadcast_to(((index_x + 0.5) / NX)[:, None, None], (NX, NY, LZ)).reshape(NX // rows_per, -1)
    node_y = jnp.broadcast_to(((index_y + 0.5) / NY)[None, :, None], (NX, NY, LZ)).reshape(NX // rows_per, -1)
    node_z = jnp.broadcast_to(((index_z + 0.5) / NZ)[None, None, :], (NX, NY, LZ)).reshape(NX // rows_per, -1)
    coef_blocks = centre_coef.reshape(NC // 256, 256, 3)
    index_blocks = centre_index.reshape(NC // 256, 256)

    def node_block(nodes):
        block_x, block_y, block_z = nodes

        def step(carry, block):
            return (carry + kernel_sum(block[0], block[1], block_x, block_y, block_z, NX, NY), None)
        totals, unused = lax.scan(step, jnp.zeros((3, block_x.shape[0]), jnp.float32), (coef_blocks, index_blocks))
        return totals
    values = lax.map(node_block, (node_x, node_y, node_z))
    rbf = jnp.transpose(values, (1, 0, 2)).reshape(3, NX, NY, LZ)
    field = jnp.concatenate([rbf, prev_disp[..., LZ:]], axis=3)
    plane_z = jnp.arange(NZ, dtype=jnp.int32)
    stiffness = stiff_factor * (float(NZ) / (plane_z.astype(jnp.float32) + 0.5))
    frozen = plane_z < LZ
    stiff_ext = jnp.pad(stiffness, 1)
    for sweep_no in range(SWEEPS):
        field_ext = jnp.pad(field, ((0, 0), (1, 1), (1, 1), (1, 1)))
        field = relax_sweep(field_ext, stiff_ext, frozen, None)
    return field
```

```python
import functools
import math

import jax
import jax.numpy as jnp
from jax import lax
from jax.experimental import pallas as pl
from jax.experimental.pallas import tpu as pltpu
from jax.sharding import PartitionSpec as P

SWEEPS = 3
RADIUS = 0.02
OMEGA = 0.8

HALO = 3
TOP = 8
WIN = 72
ROWS = 88
LANES = 128
VMEM_LIMIT = 40 * 1024 * 1024


def lane_ids(rows=WIN):
    return lax.broadcasted_iota(jnp.int32, (rows, LANES), 1)


def roll_lanes(value, shift):
    if isinstance(shift, int):
        shift = shift % LANES
        if shift == 0:
            return value
    return pltpu.roll(value, shift, 1)


def kernel_call(kernel, name, outs, flops, args, scratch=()):
    moved = sum(math.prod(a.shape) * 4 for a in (*args, *outs))
    return pl.pallas_call(
        kernel,
        name=name,
        out_shape=outs,
        in_specs=[pl.BlockSpec(memory_space=pltpu.VMEM)] * len(args),
        out_specs=tuple(pl.BlockSpec(memory_space=pltpu.VMEM) for _ in outs),
        scratch_shapes=list(scratch),
        compiler_params=pltpu.CompilerParams(vmem_limit_bytes=VMEM_LIMIT),
        cost_estimate=pl.CostEstimate(flops=flops, bytes_accessed=moved, transcendentals=0),
    )(*args)


def f32(*shape):
    return jax.ShapeDtypeStruct(shape, jnp.float32)


def pack_z_kernel(prev_ref, stiff_ref, low_ref, high_ref, ylow_ref, yhigh_ref):
    cells_x, cells_y, cells_z = stiff_ref.shape
    lane = lax.broadcasted_iota(jnp.int32, (8, LANES), 1)
    place = lane % 8
    pick = jnp.where(place <= 3, jnp.clip(3 - place, 0, 2), cells_z - 1 - jnp.clip(place - 4, 0, 2))
    for tile in range(cells_y // 8):
        rows = pl.ds(8 * tile, 8)
        edges = []
        for ch in range(4):
            edge = jnp.zeros((8, LANES), jnp.float32)
            for x in range(cells_x):
                value = prev_ref[ch, x, rows, :] if ch < 3 else stiff_ref[x, rows, :]
                picked = jnp.take_along_axis(value, pick, axis=1)
                edge = jnp.where(lane // 8 == x, picked, edge)
            edges.append(edge)
        for pair in range(2):
            even, odd = edges[2 * pair], edges[2 * pair + 1]
            low_ref[pair, rows, :] = jnp.where(place <= 3, even, roll_lanes(odd, 3))
            high_ref[pair, rows, :] = jnp.where(place >= 4, even, roll_lanes(odd, -3))
    for ch in range(4):
        for x in range(cells_x):
            at = pl.ds((ch * cells_x + x) * HALO, HALO)
            if ch < 3:
                ylow_ref[at, :] = prev_ref[ch, x, :HALO, :]
                yhigh_ref[at, :] = prev_ref[ch, x, cells_y - HALO :, :]
            else:
                ylow_ref[at, :] = stiff_ref[x, :HALO, :]
                yhigh_ref[at, :] = stiff_ref[x, cells_y - HALO :, :]


def pack_y_kernel(above_ref, below_ref, ylow_ref, yhigh_ref, edge_ref, outlow_ref, outhigh_ref):
    rows = above_ref.shape[1]
    place = lane_ids(rows) % 8
    upper = (place >= 1) & (place <= 3)
    lower = (place >= 4) & (place <= 6)
    base = ylow_ref.shape[0]
    outlow_ref[:base, :] = ylow_ref[...]
    outhigh_ref[:base, :] = yhigh_ref[...]
    for ch in range(4):
        above, below = above_ref[ch // 2], below_ref[ch // 2]
        if ch % 2:
            above, below = roll_lanes(above, -3), roll_lanes(below, 3)
        edge = jnp.where(upper, above, jnp.where(lower, below, 0.0))
        edge_ref[ch] = edge
        at = pl.ds(base + ch * HALO, HALO)
        outlow_ref[at, :] = edge[:HALO]
        outhigh_ref[at, :] = edge[rows - HALO :]
    rest = outlow_ref.shape[0] - base - 4 * HALO
    outlow_ref[base + 4 * HALO :, :] = jnp.zeros((rest, LANES), jnp.float32)
    outhigh_ref[base + 4 * HALO :, :] = jnp.zeros((rest, LANES), jnp.float32)


def pack_x_kernel(prev_ref, stiff_ref, edge_ref, yabove_ref, ybelow_ref, low_ref, high_ref, wide_ref):
    cells_x, cells_y, _ = stiff_ref.shape
    lane = lane_ids()
    base = 4 * cells_x * HALO
    rest = WIN - 2 - cells_y - HALO
    low = jnp.zeros((WIN, LANES), jnp.float32)
    high = low
    for ch in range(4):
        for p in range(HALO):
            for out, x in ((low_ref, p), (high_ref, cells_x - HALO + p)):
                at = (ch * cells_x + x) * HALO
                plane = ch * HALO + p
                out[plane, 0:2, :] = ybelow_ref[at + 1 : at + HALO, :]
                out[plane, 2 : 2 + cells_y, :] = prev_ref[ch, x] if ch < 3 else stiff_ref[x]
                out[plane, 2 + cells_y : 2 + cells_y + HALO, :] = yabove_ref[at : at + HALO, :]
                out[plane, 2 + cells_y + HALO :, :] = jnp.zeros((rest, LANES), jnp.float32)
        at = base + ch * HALO
        wide_ref[ch, 0:2, :] = ybelow_ref[at + 1 : at + HALO, :]
        wide_ref[ch, 2 : 2 + cells_y, :] = edge_ref[ch]
        wide_ref[ch, 2 + cells_y : 2 + cells_y + HALO, :] = yabove_ref[at : at + HALO, :]
        wide_ref[ch, 2 + cells_y + HALO :, :] = jnp.zeros((rest, LANES), jnp.float32)
        turned = roll_lanes(wide_ref[ch], 32 * ch)
        at_low = (lane - 32 * ch) & (LANES - 1)
        low = jnp.where(at_low < 8 * HALO, turned, low)
        high = jnp.where(at_low >= LANES - 8 * HALO, turned, high)
    low_ref[4 * HALO] = low
    high_ref[4 * HALO] = high


def stencil(count_x, count_y, count_z):
    table = {}
    for step_x in range(int(RADIUS * count_x) + 2):
        for step_y in range(int(RADIUS * count_y) + 2):
            square = (step_x / count_x) ** 2 + (step_y / count_y) ** 2 + (0.5 / count_z) ** 2
            ratio = math.sqrt(square) / RADIUS
            lead = max(1.0 - ratio, 0.0)
            if lead > 0.0:
                table[step_x, step_y] = lead**4 * (4.0 * ratio + 1.0)
    return table


REACH_X = 8
REACH_Y = 8
GRID_X = 32
GRID_Y = 80


def rbf_kernel(table, cells_x, cells_y, count_y, centres_ref, out_ref, grid_ref):
    slots = centres_ref.shape[0] // 4
    first_x = (lax.axis_index("gx") * cells_x - REACH_X).astype(jnp.float32)
    first_y = (lax.axis_index("gy") * cells_y - REACH_Y).astype(jnp.float32)
    quarter = lane_ids(slots) // 32
    fields = []
    for f in range(4):
        field = jnp.zeros((slots, LANES), jnp.float32)
        for k in range(4):
            part = roll_lanes(centres_ref[k * slots : (k + 1) * slots, :], 32 * (k - f))
            field = jnp.where(quarter == k, part, field)
        fields.append(field)
    index = fields[3]
    at_x = jnp.floor(index * (1.0 / count_y))
    at_y = index - at_x * count_y - first_y
    at_x = at_x - first_x
    heads = [f.astype(jnp.bfloat16).astype(jnp.float32) for f in fields[:3]]
    tails = [f - h for f, h in zip(fields[:3], heads)]
    row_y = lax.broadcasted_iota(jnp.int32, (GRID_Y, LANES), 0).astype(jnp.float32)
    row_x = lax.broadcasted_iota(jnp.int32, (GRID_X, LANES), 0).astype(jnp.float32)
    total = jnp.zeros((GRID_Y, 2 * LANES), jnp.float32)
    blank = jnp.zeros((LANES - 3 * GRID_X, LANES), jnp.float32)
    for q in range(0, slots, 2):
        left, right = [], []
        for r in (q, q + 1):
            hit_y = at_y[r : r + 1, :] == row_y
            hit_x = at_x[r : r + 1, :] == row_x
            left.append(jnp.where(hit_y, 1.0, 0.0).astype(jnp.bfloat16))
            pieces = []
            for group in (heads, tails):
                pieces += [jnp.where(hit_x, g[r : r + 1, :], 0.0) for g in group]
                pieces.append(blank)
            right.append(jnp.concatenate(pieces, axis=0).astype(jnp.bfloat16))
        total = total + lax.dot_general(
            jnp.concatenate(left, axis=1),
            jnp.concatenate(right, axis=1),
            (((1,), (1,)), ((), ())),
            preferred_element_type=jnp.float32,
        )
    grid = total[:, :LANES] + total[:, LANES:]
    reach_x = max(a for a, _ in table)
    reach_y = max(b for _, b in table)
    result = jnp.zeros((WIN, LANES), jnp.float32)
    for step_x in range(reach_x + 1):
        value = roll_lanes(grid, HALO - REACH_X + step_x)
        if step_x:
            value = value + roll_lanes(grid, HALO - REACH_X - step_x)
        grid_ref[:GRID_Y, :] = value
        for step_y in range(reach_y + 1):
            phi = table.get((step_x, step_y))
            if phi is None:
                continue
            start = REACH_Y - 2
            part = grid_ref[start + step_y : start + step_y + WIN, :]
            if step_y:
                part = part + grid_ref[start - step_y : start - step_y + WIN, :]
            result = result + phi * part
    for k in range(out_ref.shape[0]):
        out_ref[k] = result


def sweep_kernel(
    count_z,
    prev_ref,
    stiff_ref,
    wide_ref,
    yabove_ref,
    ybelow_ref,
    xabove_ref,
    xbelow_ref,
    rbf_ref,
    out_ref,
    u_ref,
    s_ref,
    w_ref,
    e_ref,
    es_ref,
    ew_ref,
    c_ref,
):
    cells_x, cells_y, cells_z = stiff_ref.shape
    ext = cells_x + 2 * HALO
    block_z = lax.axis_index("gz")
    window = pl.ds(TOP, WIN)
    before = pl.ds(TOP - 1, WIN)
    after = pl.ds(TOP + 1, WIN)
    lane = lane_ids()
    place = lane % 8
    group = lane // 8

    deep = (block_z * cells_z + lane_ids(1)).astype(jnp.float32) + 0.5
    scale = count_z / deep
    edge_z = jnp.where(place <= 3, cells_z + 3 - place, 3 - place)
    edge_scale = count_z / ((block_z * cells_z + edge_z).astype(jnp.float32) + 0.5)

    main = pl.ds(TOP + 2, cells_y)
    for ch in range(4):
        for x in range(cells_x):
            at = (ch * cells_x + x) * HALO
            low, high = ybelow_ref[at : at + HALO, :], yabove_ref[at : at + HALO, :]
            if ch < 3:
                u_ref[0, ch, HALO + x, main, :] = prev_ref[ch, x]
                u_ref[0, ch, HALO + x, TOP - 1 : TOP + 2, :] = low
                u_ref[0, ch, HALO + x, TOP + 2 + cells_y : TOP + 2 + cells_y + HALO, :] = high
            else:
                s_ref[HALO + x, main, :] = stiff_ref[x] * scale
                s_ref[HALO + x, TOP - 1 : TOP + 2, :] = low * scale
                s_ref[HALO + x, TOP + 2 + cells_y : TOP + 2 + cells_y + HALO, :] = high * scale
        for p in range(HALO):
            for source, x in ((xbelow_ref, p), (xabove_ref, HALO + cells_x + p)):
                if ch < 3:
                    u_ref[0, ch, x, window, :] = source[ch * HALO + p]
                else:
                    s_ref[x, window, :] = source[ch * HALO + p] * scale
        above = roll_lanes(xabove_ref[4 * HALO], -32 * ch)
        below = roll_lanes(xbelow_ref[4 * HALO], -32 * ch)
        side = jnp.where(lane < 8 * HALO, above, jnp.where(lane >= LANES - 8 * HALO, below, 0.0))
        if ch < 3:
            e_ref[0, ch, 0, window, :] = wide_ref[ch]
            e_ref[0, ch, 1, window, :] = side
        else:
            es_ref[0, window, :] = wide_ref[ch] * edge_scale
            es_ref[1, window, :] = side * edge_scale

    first = (lane == 0) & (block_z == 0)

    @pl.when(block_z == 0)
    def _():
        rbf = rbf_ref[0]
        for k in range(1, rbf_ref.shape[0]):
            rbf = rbf + rbf_ref[k]

        def layer(x, carry):
            own = first & (s_ref[x, window, :] > 0.0)
            for ch in range(3):
                column = pltpu.roll(rbf, (2 * LANES - 32 * ch - x) % LANES, 1)
                u_ref[0, ch, x, window, :] = jnp.where(own, column, u_ref[0, ch, x, window, :])
            return carry

        lax.fori_loop(0, ext, layer, 0)

    def spot(x):
        return ((x + 13) // 16 + 1) % 2, (x + 13) % 16

    def z_pair(value, edge):
        down = jnp.where(lane == 0, edge, roll_lanes(value, 1))
        up = jnp.where(lane == LANES - 1, edge, roll_lanes(value, -1))
        return down, up

    def at_edge(g):
        return (group == g) & ((place == 3) | (place == 4))

    def normalised(own, others):
        faces = [0.5 * (own + other) for other in others]
        total = functools.reduce(lambda a, b: a + b, faces)
        factor = jnp.where(own > 0.0, OMEGA / jnp.where(own > 0.0, total, 1.0), 0.0)
        return [face * factor for face in faces]

    c_ref[...] = jnp.zeros_like(c_ref)

    def weigh(x, carry):
        own = s_ref[x, window, :]
        tile, g = spot(x)
        edge = pltpu.roll(es_ref[tile, window, :], LANES - 4 - 8 * g, 1)
        down, up = z_pair(own, edge)
        others = (s_ref[x - 1, window, :], s_ref[x + 1, window, :], s_ref[x, before, :], s_ref[x, after, :], down, up)
        for k, weight in enumerate(normalised(own, others)):
            w_ref[k, x] = weight
        c_ref[0, tile] = jnp.where(at_edge(g), pltpu.roll(own, 8 * g + 4, 1), c_ref[0, tile])
        return carry

    lax.fori_loop(1, ext - 1, weigh, 0)

    def edge_neighbours(ref, tile, middle):
        own, other = ref[tile, window, :], ref[1 - tile, window, :]
        left = jnp.where(lane >= 8, roll_lanes(own, 8), roll_lanes(other, 8))
        right = jnp.where(lane < LANES - 8, roll_lanes(own, -8), roll_lanes(other, -8))
        minus = jnp.where(place == 4, middle, roll_lanes(own, 1))
        plus = jnp.where(place == 3, middle, roll_lanes(own, -1))
        return own, (left, right, ref[tile, before, :], ref[tile, after, :], minus, plus)

    for tile in range(2):
        own, others = edge_neighbours(es_ref, tile, c_ref[0, tile])
        for k, weight in enumerate(normalised(own, others)):
            ew_ref[k, tile] = weight

    for sweep in range(SWEEPS):
        now, later = sweep % 2, (sweep + 1) % 2
        last = sweep == SWEEPS - 1

        def relax(x, carry):
            tile, g = spot(x)
            weights = [w_ref[k, x] for k in range(6)]
            for ch in range(3):
                own = u_ref[now, ch, x, window, :]
                edge = pltpu.roll(e_ref[now, ch, tile, window, :], LANES - 4 - 8 * g, 1)
                down, up = z_pair(own, edge)
                others = (
                    u_ref[now, ch, x - 1, window, :],
                    u_ref[now, ch, x + 1, window, :],
                    u_ref[now, ch, x, before, :],
                    u_ref[now, ch, x, after, :],
                    down,
                    up,
                )
                new = (1.0 - OMEGA) * own
                for weight, other in zip(weights, others):
                    new = new + weight * other
                new = jnp.where(first, own, new)
                if last:
                    out_ref[ch, x - HALO] = new[2 : 2 + cells_y]
                else:
                    u_ref[later, ch, x, window, :] = new
                    c_ref[ch, tile] = jnp.where(at_edge(g), pltpu.roll(own, 8 * g + 4, 1), c_ref[ch, tile])
            return carry

        lax.fori_loop(1 + sweep, ext - 1 - sweep, relax, 0)
        if not last:
            for ch in range(3):
                for tile in range(2):
                    own, others = edge_neighbours(e_ref.at[now, ch], tile, c_ref[ch, tile])
                    new = (1.0 - OMEGA) * own
                    for k, other in enumerate(others):
                        new = new + ew_ref[k, tile] * other
                    e_ref[later, ch, tile, window, :] = new


def step(value, axis, by):
    size = lax.axis_size(axis)
    return lax.ppermute(value, axis, [(i, i + by) for i in range(size) if 0 <= i + by < size])


def body(centre_coef, centre_index, stiff_factor, prev_disp):
    cells_x, cells_y, cells_z = stiff_factor.shape
    count_x = cells_x * lax.axis_size("gx")
    count_y = cells_y * lax.axis_size("gy")
    count_z = cells_z * lax.axis_size("gz")
    blocks = lax.axis_size("gx") * lax.axis_size("gy")
    depth = lax.axis_size("gz")

    row = jnp.concatenate([centre_coef.T, centre_index.astype(jnp.float32)[None]], axis=0).reshape(1, 1, LANES)
    centres = lax.all_to_all(jnp.broadcast_to(row, (blocks, 1, LANES)), ("gx", "gy"), 0, 0, tiled=True)
    centres = centres.reshape(blocks, LANES)

    rows_y = 4 * cells_x * HALO
    low, high, ylow, yhigh = kernel_call(
        pack_z_kernel,
        "pack_z",
        (f32(2, cells_y, LANES), f32(2, cells_y, LANES), f32(rows_y, LANES), f32(rows_y, LANES)),
        1 << 21,
        (prev_disp, stiff_factor),
    )
    zabove, zbelow = step(low, "gz", -1), step(high, "gz", 1)

    table = stencil(count_x, count_y, count_z)
    (share,) = kernel_call(
        functools.partial(rbf_kernel, table, cells_x, cells_y, count_y),
        "rbf",
        (f32(depth, WIN, LANES),),
        1 << 24,
        (centres,),
        (pltpu.VMEM((ROWS, LANES), jnp.float32),),
    )
    shares = lax.all_to_all(share, "gz", 0, 0, tiled=True)

    rows_all = -(-(rows_y + 4 * HALO) // 8) * 8
    edge, ylow, yhigh = kernel_call(
        pack_y_kernel,
        "pack_y",
        (f32(4, cells_y, LANES), f32(rows_all, LANES), f32(rows_all, LANES)),
        1 << 18,
        (zabove, zbelow, ylow, yhigh),
    )
    yabove, ybelow = step(ylow, "gy", -1), step(yhigh, "gy", 1)

    xlow, xhigh, wide = kernel_call(
        pack_x_kernel,
        "pack_x",
        (f32(4 * HALO + 1, WIN, LANES), f32(4 * HALO + 1, WIN, LANES), f32(4, WIN, LANES)),
        1 << 18,
        (prev_disp, stiff_factor, edge, yabove, ybelow),
    )
    xabove, xbelow = step(xlow, "gx", -1), step(xhigh, "gx", 1)

    ext = cells_x + 2 * HALO
    (out,) = kernel_call(
        functools.partial(sweep_kernel, float(count_z)),
        "sweeps",
        (f32(3, cells_x, cells_y, LANES),),
        1 << 25,
        (prev_disp, stiff_factor, wide, yabove, ybelow, xabove, xbelow, shares),
        (
            pltpu.VMEM((2, 3, ext, ROWS, LANES), jnp.float32),
            pltpu.VMEM((ext, ROWS, LANES), jnp.float32),
            pltpu.VMEM((6, ext, WIN, LANES), jnp.float32),
            pltpu.VMEM((2, 3, 2, ROWS, LANES), jnp.float32),
            pltpu.VMEM((2, ROWS, LANES), jnp.float32),
            pltpu.VMEM((6, 2, WIN, LANES), jnp.float32),
            pltpu.VMEM((3, 2, WIN, LANES), jnp.float32),
        ),
    )
    return out


def solution(mesh):
    placed = (
        P(("gx", "gy", "gz"), None),
        P(("gx", "gy", "gz")),
        P("gx", "gy", "gz"),
        P(None, "gx", "gy", "gz"),
    )
    return jax.shard_map(
        body, mesh=mesh, in_specs=placed, out_specs=P(None, "gx", "gy", "gz"), check_vma=False
    )
```

```python
import functools
import math

import jax
import jax.numpy as jnp
from jax import lax
from jax.experimental import pallas as pl
from jax.experimental.pallas import tpu as pltpu
from jax.sharding import PartitionSpec as P

SWEEPS = 3
RADIUS = 0.02
OMEGA = 0.8

HALO = 3
TOP = 8
WIN = 72
ROWS = 88
LANES = 128
VMEM_LIMIT = 20 * 1024 * 1024


def lane_ids(rows=WIN):
    return lax.broadcasted_iota(jnp.int32, (rows, LANES), 1)


def roll_lanes(value, shift):
    if isinstance(shift, int):
        shift = shift % LANES
        if shift == 0:
            return value
    return pltpu.roll(value, shift, 1)


def kernel_call(kernel, name, outs, flops, args, scratch=(), after=(), limit=VMEM_LIMIT):
    moved = sum(math.prod(a.shape) * 4 for a in (*args, *outs))
    return pl.pallas_call(
        kernel,
        name=name,
        out_shape=outs,
        in_specs=[pl.BlockSpec(memory_space=pltpu.VMEM)] * len(args) + [pl.BlockSpec(memory_space=pl.ANY)] * len(after),
        out_specs=tuple(pl.BlockSpec(memory_space=pltpu.VMEM) for _ in outs),
        scratch_shapes=list(scratch),
        compiler_params=pltpu.CompilerParams(vmem_limit_bytes=limit),
        cost_estimate=pl.CostEstimate(flops=flops, bytes_accessed=moved, transcendentals=0),
    )(*args, *after)


def f32(*shape):
    return jax.ShapeDtypeStruct(shape, jnp.float32)


def pack_z_kernel(prev_ref, stiff_ref, low_ref, high_ref, ylow_ref, yhigh_ref):
    cells_x, cells_y, cells_z = stiff_ref.shape
    lane = lax.broadcasted_iota(jnp.int32, (8, LANES), 1)
    place = lane % 8
    pick = jnp.where(place <= 3, jnp.clip(3 - place, 0, 2), cells_z - 1 - jnp.clip(place - 4, 0, 2))
    for tile in range(cells_y // 8):
        rows = pl.ds(8 * tile, 8)
        edges = []
        for ch in range(4):
            edge = jnp.zeros((8, LANES), jnp.float32)
            for x in range(cells_x):
                value = prev_ref[ch, x, rows, :] if ch < 3 else stiff_ref[x, rows, :]
                picked = jnp.take_along_axis(value, pick, axis=1)
                edge = jnp.where(lane // 8 == x, picked, edge)
            edges.append(edge)
        for pair in range(2):
            even, odd = edges[2 * pair], edges[2 * pair + 1]
            low_ref[pair, rows, :] = jnp.where(place <= 3, even, roll_lanes(odd, 3))
            high_ref[pair, rows, :] = jnp.where(place >= 4, even, roll_lanes(odd, -3))
    for ch in range(4):
        for x in range(cells_x):
            at = pl.ds((ch * cells_x + x) * HALO, HALO)
            if ch < 3:
                ylow_ref[at, :] = prev_ref[ch, x, :HALO, :]
                yhigh_ref[at, :] = prev_ref[ch, x, cells_y - HALO :, :]
            else:
                ylow_ref[at, :] = stiff_ref[x, :HALO, :]
                yhigh_ref[at, :] = stiff_ref[x, cells_y - HALO :, :]


def pack_y_kernel(above_ref, below_ref, ylow_ref, yhigh_ref, _, edge_ref, outlow_ref, outhigh_ref):
    rows = above_ref.shape[1]
    place = lane_ids(rows) % 8
    upper = (place >= 1) & (place <= 3)
    lower = (place >= 4) & (place <= 6)
    base = ylow_ref.shape[0]
    outlow_ref[:base, :] = ylow_ref[...]
    outhigh_ref[:base, :] = yhigh_ref[...]
    for ch in range(4):
        above, below = above_ref[ch // 2], below_ref[ch // 2]
        if ch % 2:
            above, below = roll_lanes(above, -3), roll_lanes(below, 3)
        edge = jnp.where(upper, above, jnp.where(lower, below, 0.0))
        edge_ref[ch] = edge
        at = pl.ds(base + ch * HALO, HALO)
        outlow_ref[at, :] = edge[:HALO]
        outhigh_ref[at, :] = edge[rows - HALO :]
    rest = outlow_ref.shape[0] - base - 4 * HALO
    outlow_ref[base + 4 * HALO :, :] = jnp.zeros((rest, LANES), jnp.float32)
    outhigh_ref[base + 4 * HALO :, :] = jnp.zeros((rest, LANES), jnp.float32)


def pack_x_kernel(prev_ref, stiff_ref, edge_ref, yabove_ref, ybelow_ref, low_ref, high_ref, wide_ref):
    cells_x, cells_y, _ = stiff_ref.shape
    lane = lane_ids()
    base = 4 * cells_x * HALO
    rest = WIN - 2 - cells_y - HALO
    low = jnp.zeros((WIN, LANES), jnp.float32)
    high = low
    for ch in range(4):
        for p in range(HALO):
            for out, x in ((low_ref, p), (high_ref, cells_x - HALO + p)):
                at = (ch * cells_x + x) * HALO
                plane = ch * HALO + p
                out[plane, 0:2, :] = ybelow_ref[at + 1 : at + HALO, :]
                out[plane, 2 : 2 + cells_y, :] = prev_ref[ch, x] if ch < 3 else stiff_ref[x]
                out[plane, 2 + cells_y : 2 + cells_y + HALO, :] = yabove_ref[at : at + HALO, :]
                out[plane, 2 + cells_y + HALO :, :] = jnp.zeros((rest, LANES), jnp.float32)
        at = base + ch * HALO
        wide_ref[ch, 0:2, :] = ybelow_ref[at + 1 : at + HALO, :]
        wide_ref[ch, 2 : 2 + cells_y, :] = edge_ref[ch]
        wide_ref[ch, 2 + cells_y : 2 + cells_y + HALO, :] = yabove_ref[at : at + HALO, :]
        wide_ref[ch, 2 + cells_y + HALO :, :] = jnp.zeros((rest, LANES), jnp.float32)
        turned = roll_lanes(wide_ref[ch], 32 * ch)
        at_low = (lane - 32 * ch) & (LANES - 1)
        low = jnp.where(at_low < 8 * HALO, turned, low)
        high = jnp.where(at_low >= LANES - 8 * HALO, turned, high)
    low_ref[4 * HALO] = low
    high_ref[4 * HALO] = high


def stencil(count_x, count_y, count_z):
    table = {}
    for step_x in range(int(RADIUS * count_x) + 2):
        for step_y in range(int(RADIUS * count_y) + 2):
            square = (step_x / count_x) ** 2 + (step_y / count_y) ** 2 + (0.5 / count_z) ** 2
            ratio = math.sqrt(square) / RADIUS
            lead = max(1.0 - ratio, 0.0)
            if lead > 0.0:
                table[step_x, step_y] = lead**4 * (4.0 * ratio + 1.0)
    return table


REACH_X = 8
REACH_Y = 8
GRID_X = 32
GRID_Y = 80


def rbf_kernel(table, cells_x, cells_y, count_y, centres_ref, out_ref, grid_ref):
    slots = centres_ref.shape[0] // 4
    first_x = (lax.axis_index("gx") * cells_x - REACH_X).astype(jnp.float32)
    first_y = (lax.axis_index("gy") * cells_y - REACH_Y).astype(jnp.float32)
    quarter = lane_ids(slots) // 32
    fields = []
    for f in range(4):
        field = jnp.zeros((slots, LANES), jnp.float32)
        for k in range(4):
            part = roll_lanes(centres_ref[k * slots : (k + 1) * slots, :], 32 * (k - f))
            field = jnp.where(quarter == k, part, field)
        fields.append(field)
    index = fields[3]
    at_x = jnp.floor(index * (1.0 / count_y))
    at_y = index - at_x * count_y - first_y
    at_x = at_x - first_x
    heads = [f.astype(jnp.bfloat16).astype(jnp.float32) for f in fields[:3]]
    tails = [f - h for f, h in zip(fields[:3], heads)]
    row_y = lax.broadcasted_iota(jnp.int32, (GRID_Y, LANES), 0).astype(jnp.float32)
    row_x = lax.broadcasted_iota(jnp.int32, (GRID_X, LANES), 0).astype(jnp.float32)
    total = jnp.zeros((GRID_Y, 2 * LANES), jnp.float32)
    blank = jnp.zeros((LANES - 3 * GRID_X, LANES), jnp.float32)
    for q in range(0, slots, 2):
        left, right = [], []
        for r in (q, q + 1):
            hit_y = at_y[r : r + 1, :] == row_y
            hit_x = at_x[r : r + 1, :] == row_x
            left.append(jnp.where(hit_y, 1.0, 0.0).astype(jnp.bfloat16))
            pieces = []
            for group in (heads, tails):
                pieces += [jnp.where(hit_x, g[r : r + 1, :], 0.0) for g in group]
                pieces.append(blank)
            right.append(jnp.concatenate(pieces, axis=0).astype(jnp.bfloat16))
        total = total + lax.dot_general(
            jnp.concatenate(left, axis=1),
            jnp.concatenate(right, axis=1),
            (((1,), (1,)), ((), ())),
            preferred_element_type=jnp.float32,
        )
    grid = total[:, :LANES] + total[:, LANES:]
    reach_x = max(a for a, _ in table)
    reach_y = max(b for _, b in table)
    result = jnp.zeros((WIN, LANES), jnp.float32)
    for step_x in range(reach_x + 1):
        value = roll_lanes(grid, HALO - REACH_X + step_x)
        if step_x:
            value = value + roll_lanes(grid, HALO - REACH_X - step_x)
        grid_ref[:GRID_Y, :] = value
        for step_y in range(reach_y + 1):
            phi = table.get((step_x, step_y))
            if phi is None:
                continue
            start = REACH_Y - 2
            part = grid_ref[start + step_y : start + step_y + WIN, :]
            if step_y:
                part = part + grid_ref[start - step_y : start - step_y + WIN, :]
            result = result + phi * part
    for k in range(out_ref.shape[0]):
        out_ref[k] = result


def sweep_kernel(
    count_z,
    prev_ref,
    stiff_ref,
    wide_ref,
    yabove_ref,
    ybelow_ref,
    xabove_ref,
    xbelow_ref,
    rbf_ref,
    out_ref,
    u_ref,
    s_ref,
    w_ref,
    e_ref,
    es_ref,
    ew_ref,
    c_ref,
):
    cells_x, cells_y, cells_z = stiff_ref.shape
    ext = cells_x + 2 * HALO
    block_z = lax.axis_index("gz")
    window = pl.ds(TOP, WIN)
    before = pl.ds(TOP - 1, WIN)
    after = pl.ds(TOP + 1, WIN)
    lane = lane_ids()
    place = lane % 8
    group = lane // 8

    deep = (block_z * cells_z + lane_ids(1)).astype(jnp.float32) + 0.5
    scale = count_z / deep
    edge_z = jnp.where(place <= 3, cells_z + 3 - place, 3 - place)
    edge_scale = count_z / ((block_z * cells_z + edge_z).astype(jnp.float32) + 0.5)

    main = pl.ds(TOP + 2, cells_y)
    for ch in range(4):
        for x in range(cells_x):
            at = (ch * cells_x + x) * HALO
            low, high = ybelow_ref[at : at + HALO, :], yabove_ref[at : at + HALO, :]
            if ch < 3:
                u_ref[0, ch, HALO + x, main, :] = prev_ref[ch, x]
                u_ref[0, ch, HALO + x, TOP - 1 : TOP + 2, :] = low
                u_ref[0, ch, HALO + x, TOP + 2 + cells_y : TOP + 2 + cells_y + HALO, :] = high
            else:
                s_ref[HALO + x, main, :] = stiff_ref[x] * scale
                s_ref[HALO + x, TOP - 1 : TOP + 2, :] = low * scale
                s_ref[HALO + x, TOP + 2 + cells_y : TOP + 2 + cells_y + HALO, :] = high * scale
        for p in range(HALO):
            for source, x in ((xbelow_ref, p), (xabove_ref, HALO + cells_x + p)):
                if ch < 3:
                    u_ref[0, ch, x, window, :] = source[ch * HALO + p]
                else:
                    s_ref[x, window, :] = source[ch * HALO + p] * scale
        above = roll_lanes(xabove_ref[4 * HALO], -32 * ch)
        below = roll_lanes(xbelow_ref[4 * HALO], -32 * ch)
        side = jnp.where(lane < 8 * HALO, above, jnp.where(lane >= LANES - 8 * HALO, below, 0.0))
        if ch < 3:
            e_ref[0, ch, 0, window, :] = wide_ref[ch]
            e_ref[0, ch, 1, window, :] = side
        else:
            es_ref[0, window, :] = wide_ref[ch] * edge_scale
            es_ref[1, window, :] = side * edge_scale

    first = (lane == 0) & (block_z == 0)

    @pl.when(block_z == 0)
    def _():
        rbf = rbf_ref[0]
        for k in range(1, rbf_ref.shape[0]):
            rbf = rbf + rbf_ref[k]

        def layer(x, carry):
            own = first & (s_ref[x, window, :] > 0.0)
            for ch in range(3):
                column = pltpu.roll(rbf, (2 * LANES - 32 * ch - x) % LANES, 1)
                u_ref[0, ch, x, window, :] = jnp.where(own, column, u_ref[0, ch, x, window, :])
            return carry

        lax.fori_loop(0, ext, layer, 0, unroll=11)

    def spot(x):
        return ((x + 13) // 16 + 1) % 2, (x + 13) % 16

    def z_pair(value, edge):
        down = jnp.where(lane == 0, edge, roll_lanes(value, 1))
        up = jnp.where(lane == LANES - 1, edge, roll_lanes(value, -1))
        return down, up

    def at_edge(g):
        return (group == g) & ((place == 3) | (place == 4))

    def normalised(own, others):
        faces = [0.5 * (own + other) for other in others]
        total = functools.reduce(lambda a, b: a + b, faces)
        factor = jnp.where(own > 0.0, OMEGA / jnp.where(own > 0.0, total, 1.0), 0.0)
        return [face * factor for face in faces]

    c_ref[...] = jnp.zeros_like(c_ref)

    def weigh(x, carry):
        own = s_ref[x, window, :]
        tile, g = spot(x)
        edge = pltpu.roll(es_ref[tile, window, :], LANES - 4 - 8 * g, 1)
        down, up = z_pair(own, edge)
        others = (s_ref[x - 1, window, :], s_ref[x + 1, window, :], s_ref[x, before, :], s_ref[x, after, :], down, up)
        for k, weight in enumerate(normalised(own, others)):
            w_ref[k, x] = weight
        c_ref[0, tile] = jnp.where(at_edge(g), pltpu.roll(own, 8 * g + 4, 1), c_ref[0, tile])
        return carry

    lax.fori_loop(1, ext - 1, weigh, 0, unroll=4)

    def edge_neighbours(ref, tile, middle):
        own, other = ref[tile, window, :], ref[1 - tile, window, :]
        left = jnp.where(lane >= 8, roll_lanes(own, 8), roll_lanes(other, 8))
        right = jnp.where(lane < LANES - 8, roll_lanes(own, -8), roll_lanes(other, -8))
        minus = jnp.where(place == 4, middle, roll_lanes(own, 1))
        plus = jnp.where(place == 3, middle, roll_lanes(own, -1))
        return own, (left, right, ref[tile, before, :], ref[tile, after, :], minus, plus)

    for tile in range(2):
        own, others = edge_neighbours(es_ref, tile, c_ref[0, tile])
        for k, weight in enumerate(normalised(own, others)):
            ew_ref[k, tile] = weight

    for sweep in range(SWEEPS):
        now, later = sweep % 2, (sweep + 1) % 2
        last = sweep == SWEEPS - 1

        def relax(x, carry):
            tile, g = spot(x)
            weights = [w_ref[k, x] for k in range(6)]
            for ch in range(3):
                own = u_ref[now, ch, x, window, :]
                edge = pltpu.roll(e_ref[now, ch, tile, window, :], LANES - 4 - 8 * g, 1)
                down, up = z_pair(own, edge)
                others = (
                    u_ref[now, ch, x - 1, window, :],
                    u_ref[now, ch, x + 1, window, :],
                    u_ref[now, ch, x, before, :],
                    u_ref[now, ch, x, after, :],
                    down,
                    up,
                )
                new = (1.0 - OMEGA) * own
                for weight, other in zip(weights, others):
                    new = new + weight * other
                new = jnp.where(first, own, new)
                if last:
                    out_ref[ch, x - HALO] = new[2 : 2 + cells_y]
                else:
                    u_ref[later, ch, x, window, :] = new
                    c_ref[ch, tile] = jnp.where(at_edge(g), pltpu.roll(own, 8 * g + 4, 1), c_ref[ch, tile])
            return carry

        lax.fori_loop(1 + sweep, ext - 1 - sweep, relax, 0, unroll=4)
        if not last:
            for ch in range(3):
                for tile in range(2):
                    own, others = edge_neighbours(e_ref.at[now, ch], tile, c_ref[ch, tile])
                    new = (1.0 - OMEGA) * own
                    for k, other in enumerate(others):
                        new = new + ew_ref[k, tile] * other
                    e_ref[later, ch, tile, window, :] = new


def step(value, axis, by):
    size = lax.axis_size(axis)
    return lax.ppermute(value, axis, [(i, i + by) for i in range(size) if 0 <= i + by < size])


def body(centre_coef, centre_index, stiff_factor, prev_disp):
    cells_x, cells_y, cells_z = stiff_factor.shape
    count_x = cells_x * lax.axis_size("gx")
    count_y = cells_y * lax.axis_size("gy")
    count_z = cells_z * lax.axis_size("gz")
    blocks = lax.axis_size("gx") * lax.axis_size("gy")
    depth = lax.axis_size("gz")

    row = jnp.concatenate([centre_coef.T, centre_index.astype(jnp.float32)[None]], axis=0).reshape(1, 1, LANES)
    centres = lax.all_to_all(jnp.broadcast_to(row, (blocks, 1, LANES)), ("gx", "gy"), 0, 0, tiled=True)
    centres = centres.reshape(blocks, LANES)

    rows_y = 4 * cells_x * HALO
    low, high, ylow, yhigh = kernel_call(
        pack_z_kernel,
        "pack_z",
        (f32(2, cells_y, LANES), f32(2, cells_y, LANES), f32(rows_y, LANES), f32(rows_y, LANES)),
        1 << 21,
        (prev_disp, stiff_factor),
    )
    zabove, zbelow = step(low, "gz", -1), step(high, "gz", 1)

    table = stencil(count_x, count_y, count_z)
    (share,) = kernel_call(
        functools.partial(rbf_kernel, table, cells_x, cells_y, count_y),
        "rbf",
        (f32(depth, WIN, LANES),),
        1 << 24,
        (centres,),
        (pltpu.VMEM((ROWS, LANES), jnp.float32),),
    )
    shares = lax.all_to_all(share, "gz", 0, 0, tiled=True)

    rows_all = -(-(rows_y + 4 * HALO) // 8) * 8
    edge, ylow, yhigh = kernel_call(
        pack_y_kernel,
        "pack_y",
        (f32(4, cells_y, LANES), f32(rows_all, LANES), f32(rows_all, LANES)),
        1 << 18,
        (zabove, zbelow, ylow, yhigh),
        after=(share,),
    )
    yabove, ybelow = step(ylow, "gy", -1), step(yhigh, "gy", 1)

    xlow, xhigh, wide = kernel_call(
        pack_x_kernel,
        "pack_x",
        (f32(4 * HALO + 1, WIN, LANES), f32(4 * HALO + 1, WIN, LANES), f32(4, WIN, LANES)),
        1 << 18,
        (prev_disp, stiff_factor, edge, yabove, ybelow),
    )
    xabove, xbelow = step(xlow, "gx", -1), step(xhigh, "gx", 1)

    ext = cells_x + 2 * HALO
    (out,) = kernel_call(
        functools.partial(sweep_kernel, float(count_z)),
        "sweeps",
        (f32(3, cells_x, cells_y, LANES),),
        1 << 25,
        (prev_disp, stiff_factor, wide, yabove, ybelow, xabove, xbelow, shares),
        (
            pltpu.VMEM((2, 3, ext, ROWS, LANES), jnp.float32),
            pltpu.VMEM((ext, ROWS, LANES), jnp.float32),
            pltpu.VMEM((6, ext, WIN, LANES), jnp.float32),
            pltpu.VMEM((2, 3, 2, ROWS, LANES), jnp.float32),
            pltpu.VMEM((2, ROWS, LANES), jnp.float32),
            pltpu.VMEM((6, 2, WIN, LANES), jnp.float32),
            pltpu.VMEM((3, 2, WIN, LANES), jnp.float32),
        ),
    )
    return out


def solution(mesh):
    placed = (
        P(("gx", "gy", "gz"), None),
        P(("gx", "gy", "gz")),
        P("gx", "gy", "gz"),
        P(None, "gx", "gy", "gz"),
    )
    return jax.shard_map(
        body, mesh=mesh, in_specs=placed, out_specs=P(None, "gx", "gy", "gz"), check_vma=False
    )
```

```python
import functools
import math

import jax
import jax.numpy as jnp
from jax import lax
from jax.experimental import pallas as pl
from jax.experimental.pallas import tpu as pltpu
from jax.sharding import PartitionSpec as P

SWEEPS = 3
RADIUS = 0.02
OMEGA = 0.8

HALO = 3
TOP = 8
WIN = 72
HALF = 40
ROWS = 88
LANES = 128
MEGA = 1_100_000
VMEM_LIMIT = 16 * 1024 * 1024


def lane_ids(rows=WIN):
    return lax.broadcasted_iota(jnp.int32, (rows, LANES), 1)


def roll_lanes(value, shift):
    if not isinstance(shift, int):
        return pltpu.roll(value, shift % LANES, 1)
    return pltpu.roll(value, shift % LANES, 1) if shift % LANES else value


def kernel_call(kernel, name, outs, flops, args, scratch=(), after=(), far=(), aliases=None):
    moved = sum(math.prod(a.shape) * 4 for a in (*args, *outs))
    anywhere = pl.BlockSpec(memory_space=pl.ANY)
    return pl.pallas_call(
        kernel,
        name=name,
        out_shape=outs,
        in_specs=[pl.BlockSpec(memory_space=pltpu.VMEM)] * len(args) + [anywhere] * (len(far) + len(after)),
        out_specs=tuple(anywhere if isinstance(o, Far) else pl.BlockSpec(memory_space=pltpu.VMEM) for o in outs),
        scratch_shapes=list(scratch),
        input_output_aliases=aliases or {},
        compiler_params=pltpu.CompilerParams(vmem_limit_bytes=VMEM_LIMIT),
        cost_estimate=pl.CostEstimate(flops=flops, bytes_accessed=moved, transcendentals=0),
    )(*args, *far, *after)


class Far(jax.ShapeDtypeStruct):
    pass


def f32(*shape):
    return jax.ShapeDtypeStruct(shape, jnp.float32)


def near(*shape):
    return pltpu.VMEM(shape, jnp.float32)


def wall_scale(count_z, cells_z):
    deep = (lax.axis_index("gz") * cells_z + lane_ids(1)).astype(jnp.float32) + 0.5
    return count_z / deep


def begin_kernel(
    count_z,
    coef_ref,
    index_ref,
    prev_ref,
    stiff_ref,
    rows_ref,
    low_ref,
    high_ref,
    ylow_ref,
    yhigh_ref,
    prevv_ref,
    raw_ref,
    edge_ref,
    sems,
):
    _, cells_x, cells_y, cells_z = prevv_ref.shape
    copies = [pltpu.make_async_copy(prev_ref.at[ch], prevv_ref.at[ch], sems.at[ch]) for ch in range(3)]
    copies.append(pltpu.make_async_copy(stiff_ref, raw_ref, sems.at[3]))
    for copy in copies:
        copy.start()
    row = jnp.concatenate(
        [coef_ref[f : f + 1, :] for f in range(3)] + [index_ref[...].astype(jnp.float32)], axis=1
    )
    rows_ref[...] = jnp.broadcast_to(row, rows_ref.shape)
    scale = wall_scale(count_z, cells_z)
    lane = lax.broadcasted_iota(jnp.int32, (8, LANES), 1)
    place = lane % 8
    pick = jnp.where(place <= 3, jnp.clip(3 - place, 0, 2), cells_z - 1 - jnp.clip(place - 4, 0, 2))
    for ch in range(4):
        copies[ch].wait()
        for tile in range(cells_y // 8):
            rows = pl.ds(8 * tile, 8)
            edge = jnp.zeros((8, LANES), jnp.float32)
            for x in range(cells_x):
                if ch < 3:
                    value = prevv_ref[ch, x, rows, :]
                else:
                    value = raw_ref[x, rows, :] * scale
                picked = jnp.take_along_axis(value, pick, axis=1)
                edge = jnp.where(lane // 8 == x, picked, edge)
            edge_ref[ch, rows, :] = edge
        for x in range(cells_x):
            at = pl.ds((ch * cells_x + x) * HALO, HALO)
            plane = prevv_ref.at[ch, x] if ch < 3 else raw_ref.at[x]
            factor = 1.0 if ch < 3 else scale
            ylow_ref[at, :] = plane[:HALO, :] * factor
            yhigh_ref[at, :] = plane[cells_y - HALO :, :] * factor
    place = lane_ids(cells_y) % 8
    for pair in range(2):
        even, odd = edge_ref[2 * pair], edge_ref[2 * pair + 1]
        low_ref[pair] = jnp.where(place <= 3, even, roll_lanes(odd, 3))
        high_ref[pair] = jnp.where(place >= 4, even, roll_lanes(odd, -3))


def pack_y_kernel(above_ref, below_ref, ylow_ref, yhigh_ref, _, edge_ref, outlow_ref, outhigh_ref):
    rows = above_ref.shape[1]
    place = lane_ids(rows) % 8
    upper = (place >= 1) & (place <= 3)
    lower = (place >= 4) & (place <= 6)
    base = ylow_ref.shape[0]
    outlow_ref[:base, :] = ylow_ref[...]
    outhigh_ref[:base, :] = yhigh_ref[...]
    for ch in range(4):
        above, below = above_ref[ch // 2], below_ref[ch // 2]
        if ch % 2:
            above, below = roll_lanes(above, -3), roll_lanes(below, 3)
        edge = jnp.where(upper, above, jnp.where(lower, below, 0.0))
        edge_ref[ch] = edge
        at = pl.ds(base + ch * HALO, HALO)
        outlow_ref[at, :] = edge[:HALO]
        outhigh_ref[at, :] = edge[rows - HALO :]
    rest = outlow_ref.shape[0] - base - 4 * HALO
    outlow_ref[base + 4 * HALO :, :] = jnp.zeros((rest, LANES), jnp.float32)
    outhigh_ref[base + 4 * HALO :, :] = jnp.zeros((rest, LANES), jnp.float32)


def fill(out, below_ref, middle, above_ref, at):
    cells_y = middle.shape[0]
    out[0:2, :] = below_ref[at + 1 : at + HALO, :]
    out[2 : 2 + cells_y, :] = middle
    out[2 + cells_y : 2 + cells_y + HALO, :] = above_ref[at : at + HALO, :]
    out[2 + cells_y + HALO : WIN, :] = jnp.zeros((WIN - 2 - cells_y - HALO, LANES), jnp.float32)


def pack_x_kernel(
    count_z, edge_ref, yabove_ref, ybelow_ref, prev_ref, stiff_ref, low_ref, high_ref, faces_ref, wide_ref, sems
):
    _, cells_x, cells_y, cells_z = prev_ref.shape
    copies = []
    for side, x in enumerate((0, cells_x - HALO)):
        for ch in range(4):
            source = prev_ref.at[ch, pl.ds(x, HALO)] if ch < 3 else stiff_ref.at[pl.ds(x, HALO)]
            copies.append(pltpu.make_async_copy(source, faces_ref.at[side, ch], sems.at[side, ch]))
    for copy in copies:
        copy.start()
    scale = wall_scale(count_z, cells_z)
    lane = lane_ids()
    base = 4 * cells_x * HALO
    low = jnp.zeros((WIN, LANES), jnp.float32)
    high = low

    for ch in range(4):
        fill(wide_ref.at[ch], ybelow_ref, edge_ref[ch], yabove_ref, base + ch * HALO)
        turned = roll_lanes(wide_ref[ch], 32 * ch)
        at_low = (lane - 32 * ch) & (LANES - 1)
        low = jnp.where(at_low < 8 * HALO, turned, low)
        high = jnp.where(at_low >= LANES - 8 * HALO, turned, high)
    low_ref[4 * HALO] = low
    high_ref[4 * HALO] = high
    for copy in copies:
        copy.wait()
    for side, out in enumerate((low_ref, high_ref)):
        for ch in range(4):
            for p in range(HALO):
                x = p + side * (cells_x - HALO)
                middle = faces_ref[side, ch, p] * (1.0 if ch < 3 else scale)
                fill(out.at[ch * HALO + p], ybelow_ref, middle, yabove_ref, (ch * cells_x + x) * HALO)


def stencil(count_x, count_y, count_z):
    table = {}
    for step_x in range(int(RADIUS * count_x) + 2):
        for step_y in range(int(RADIUS * count_y) + 2):
            square = (step_x / count_x) ** 2 + (step_y / count_y) ** 2 + (0.5 / count_z) ** 2
            ratio = math.sqrt(square) / RADIUS
            lead = max(1.0 - ratio, 0.0)
            if lead > 0.0:
                table[step_x, step_y] = lead**4 * (4.0 * ratio + 1.0)
    return table


REACH_X = 8
REACH_Y = 8
GRID_X = 32
GRID_Y = 80


def rbf_kernel(table, cells_x, cells_y, count_y, centres_ref, out_ref, grid_ref):
    slots = centres_ref.shape[0] // 4
    first_x = (lax.axis_index("gx") * cells_x - REACH_X).astype(jnp.float32)
    first_y = (lax.axis_index("gy") * cells_y - REACH_Y).astype(jnp.float32)
    quarter = lane_ids(slots) // 32
    fields = []
    for f in range(4):
        field = jnp.zeros((slots, LANES), jnp.float32)
        for k in range(4):
            part = roll_lanes(centres_ref[k * slots : (k + 1) * slots, :], 32 * (k - f))
            field = jnp.where(quarter == k, part, field)
        fields.append(field)
    index = fields[3]
    at_x = jnp.floor(index * (1.0 / count_y))
    at_y = index - at_x * count_y - first_y
    at_x = at_x - first_x
    heads = [f.astype(jnp.bfloat16).astype(jnp.float32) for f in fields[:3]]
    tails = [f - h for f, h in zip(fields[:3], heads)]
    row_y = lax.broadcasted_iota(jnp.int32, (GRID_Y, LANES), 0).astype(jnp.float32)
    row_x = lax.broadcasted_iota(jnp.int32, (GRID_X, LANES), 0).astype(jnp.float32)
    total = jnp.zeros((GRID_Y, 2 * LANES), jnp.float32)
    blank = jnp.zeros((LANES - 3 * GRID_X, LANES), jnp.float32)
    for q in range(0, slots, 2):
        left, right = [], []
        for r in (q, q + 1):
            hit_y = at_y[r : r + 1, :] == row_y
            hit_x = at_x[r : r + 1, :] == row_x
            left.append(jnp.where(hit_y, 1.0, 0.0).astype(jnp.bfloat16))
            pieces = []
            for group in (heads, tails):
                pieces += [jnp.where(hit_x, g[r : r + 1, :], 0.0) for g in group]
                pieces.append(blank)
            right.append(jnp.concatenate(pieces, axis=0).astype(jnp.bfloat16))
        total = total + lax.dot_general(
            jnp.concatenate(left, axis=1),
            jnp.concatenate(right, axis=1),
            (((1,), (1,)), ((), ())),
            preferred_element_type=jnp.float32,
        )
    grid = total[:, :LANES] + total[:, LANES:]
    reach_x = max(a for a, _ in table)
    reach_y = max(b for _, b in table)
    result = jnp.zeros((WIN, LANES), jnp.float32)
    for step_x in range(reach_x + 1):
        value = roll_lanes(grid, 2 - REACH_X + step_x)
        if step_x:
            value = value + roll_lanes(grid, 2 - REACH_X - step_x)
        grid_ref[:GRID_Y, :] = value
        for step_y in range(reach_y + 1):
            phi = table.get((step_x, step_y))
            if phi is None:
                continue
            start = REACH_Y - 2
            part = grid_ref[start + step_y : start + step_y + WIN, :]
            if step_y:
                part = part + grid_ref[start - step_y : start - step_y + WIN, :]
            result = result + phi * part
    lane = lane_ids()
    width = cells_x + 4
    close = jnp.where(
        lane < width,
        result,
        jnp.where(lane < 2 * width, roll_lanes(result, width - 32), roll_lanes(result, 2 * (width - 32))),
    )
    half = out_ref.shape[1]
    share = jnp.where(lane_ids(half) < LANES // 2, close[:half], roll_lanes(close[WIN - half :], LANES // 2))
    for k in range(out_ref.shape[0]):
        out_ref[k] = share


WINDOW = pl.ds(TOP, WIN)
BEFORE = pl.ds(TOP - 1, WIN)
AFTER = pl.ds(TOP + 1, WIN)


def spot(x):
    if isinstance(x, int):
        return (0 if 0 <= x < 16 else 1), x % 16
    return 0, x


def beside(value, edge):
    lane = lane_ids()
    down = jnp.where(lane == 0, edge, roll_lanes(value, 1))
    up = jnp.where(lane == LANES - 1, edge, roll_lanes(value, -1))
    return down, up


def from_edge(tile, g):
    return roll_lanes(tile, LANES - 4 - 8 * g)


def to_edge(old, plane, g):
    lane = lane_ids()
    here = (lane // 8 == g) & ((lane % 8 == 3) | (lane % 8 == 4))
    return jnp.where(here, roll_lanes(plane, 8 * g + 4), old)


def beside_edge(own_ref, other, middle):
    lane = lane_ids()
    place = lane % 8
    own = own_ref[WINDOW, :]
    left = jnp.where(lane >= 8, roll_lanes(own, 8), roll_lanes(other, 8))
    right = jnp.where(lane < LANES - 8, roll_lanes(own, -8), roll_lanes(other, -8))
    minus = jnp.where(place == 4, middle, roll_lanes(own, 1))
    plus = jnp.where(place == 3, middle, roll_lanes(own, -1))
    return left, right, own_ref[BEFORE, :], own_ref[AFTER, :], minus, plus


def normalised(own, others):
    faces = [0.5 * (own + other) for other in others]
    total = functools.reduce(lambda a, b: a + b, faces)
    inside = own > 0.0
    factor = jnp.where(inside, OMEGA / jnp.where(inside, total, 1.0), 0.0)
    return [face * factor for face in faces]


def relaxed(own, others, weights):
    new = (1.0 - OMEGA) * own
    for weight, other in zip(weights, others):
        new = new + weight * other
    return new


def zeros():
    return jnp.zeros((WIN, LANES), jnp.float32)


def wall_lane():
    return (lane_ids() == 0) & (lax.axis_index("gz") == 0)


def column_of(rbf, ch, x, cells_x):
    return roll_lanes(rbf, 2 * LANES - 2 - (cells_x + 4) * ch - x)


def inner_kernel(
    count_z, prev_ref, stiff_ref, edge_ref, yabove_ref, ybelow_ref, shares_ref,
    u0_ref, u1_ref, u2_ref, s_ref, w_ref, es_ref, cs_ref, c_ref, rbf_ref, widev_ref, out_ref,
    prevv_ref, raw_ref, own_ref, above_ref, below_ref, parts_ref, e_ref, ew_ref, done_ref, sems,
):
    _, cells_x, cells_y, cells_z = prevv_ref.shape
    fetched = ((stiff_ref, raw_ref), (yabove_ref, above_ref), (ybelow_ref, below_ref), (edge_ref, own_ref),
               (prev_ref, prevv_ref), (shares_ref, parts_ref))
    copies = [pltpu.make_async_copy(a, b, sems.at[k]) for k, (a, b) in enumerate(fetched)]
    for copy in copies:
        copy.start()
    first = wall_lane()
    scale = wall_scale(count_z, cells_z)
    main = pl.ds(TOP + 2, cells_y)

    def assemble(ch, x):
        at = (ch * cells_x + x) * HALO
        plane = u0_ref.at[ch, x] if ch < 3 else s_ref.at[x]
        plane[main, :] = prevv_ref[ch, x] if ch < 3 else raw_ref[x] * scale
        plane[TOP - 1 : TOP + 2, :] = below_ref[at : at + HALO, :]
        plane[TOP + 2 + cells_y : TOP + 2 + cells_y + HALO, :] = above_ref[at : at + HALO, :]

    for copy in copies[:4]:
        copy.wait()
    for x in range(cells_x):
        assemble(3, x)
    for ch in range(4):
        fill(widev_ref.at[ch], below_ref, own_ref[ch], above_ref, (4 * cells_x + ch) * HALO)
    es_ref[WINDOW, :] = widev_ref[3]
    cs_ref[...] = zeros()
    for x in (0, cells_x - 1):
        cs_ref[...] = to_edge(cs_ref[...], s_ref[x, WINDOW, :], x)

    def weigh(x, carry):
        own = s_ref[x, WINDOW, :]
        down, up = beside(own, from_edge(es_ref[WINDOW, :], x))
        others = (s_ref[x - 1, WINDOW, :], s_ref[x + 1, WINDOW, :], s_ref[x, BEFORE, :], s_ref[x, AFTER, :], down, up)
        for k, weight in enumerate(normalised(own, others)):
            w_ref[k, x] = weight
        cs_ref[...] = to_edge(cs_ref[...], own, x)
        return carry

    lax.fori_loop(1, cells_x - 1, weigh, 0, unroll=14)
    others = beside_edge(es_ref, zeros(), cs_ref[...])
    for k, weight in enumerate(normalised(es_ref[WINDOW, :], others)):
        ew_ref[k] = weight

    for copy in copies[4:]:
        copy.wait()
    for ch in range(3):
        e_ref[0, ch, WINDOW, :] = widev_ref[ch]
        for x in range(cells_x):
            assemble(ch, x)
    rbf_ref[...] = zeros()

    @pl.when(lax.axis_index("gz") == 0)
    def _():
        share = parts_ref[0]
        for k in range(1, parts_ref.shape[0]):
            share = share + parts_ref[k]
        half = share.shape[0]
        rbf_ref[WIN - half :, :] = roll_lanes(share, LANES // 2)
        rbf_ref[:half, :] = share
        rbf = rbf_ref[...]

        def layer(x, carry):
            own = first & (s_ref[x, WINDOW, :] > 0.0)
            for ch in range(3):
                column = column_of(rbf, ch, x, cells_x)
                u0_ref[ch, x, WINDOW, :] = jnp.where(own, column, u0_ref[ch, x, WINDOW, :])
            return carry

        lax.fori_loop(0, cells_x, layer, 0, unroll=16)

    for ch in range(3):
        ends = zeros()
        for x in range(cells_x):
            ends = to_edge(ends, u0_ref[ch, x, WINDOW, :], x)
        c_ref[0, ch] = ends
        c_ref[1, ch] = zeros()

    stages = (u0_ref, u1_ref, u2_ref)
    for sweep in range(SWEEPS):
        now, last = stages[sweep], sweep == SWEEPS - 1

        def relax(x, carry):
            weights = [w_ref[k, x] for k in range(6)]
            for ch in range(3):
                own = now[ch, x, WINDOW, :]
                down, up = beside(own, from_edge(e_ref[sweep, ch, WINDOW, :], x))
                others = (
                    now[ch, x - 1, WINDOW, :],
                    now[ch, x + 1, WINDOW, :],
                    now[ch, x, BEFORE, :],
                    now[ch, x, AFTER, :],
                    down,
                    up,
                )
                new = jnp.where(first, own, relaxed(own, others, weights))
                if last:
                    done_ref[ch, x] = new[2 : 2 + cells_y]
                else:
                    stages[sweep + 1][ch, x, WINDOW, :] = new
                if sweep == 0:
                    c_ref[1, ch] = to_edge(c_ref[1, ch], new, x)
            return carry

        lax.fori_loop(1 + sweep, cells_x - 1 - sweep, relax, 0, unroll=(14, 12, 10)[sweep])
        if not last:
            for ch in range(3):
                others = beside_edge(e_ref.at[sweep, ch], zeros(), c_ref[sweep, ch])
                weights = [ew_ref[k] for k in range(6)]
                e_ref[sweep + 1, ch, WINDOW, :] = relaxed(e_ref[sweep, ch, WINDOW, :], others, weights)
    inside = pl.ds(HALO, cells_x - 2 * HALO)
    copies = [
        pltpu.make_async_copy(done_ref.at[ch, inside], out_ref.at[ch, inside], sems.at[6 + ch]) for ch in range(3)
    ]
    for copy in copies:
        copy.start()
    for copy in copies:
        copy.wait()


def outer_kernel(
    u0_ref, u1_ref, u2_ref, s_ref, w_ref, wide_ref, es_ref, cs_ref, c_ref, rbf_ref, xabove_ref, xbelow_ref, _,
    out_ref,
    h0_ref, h1_ref, h2_ref, hs_ref, hw_ref, e_ref, eside_ref, ew_ref, c1_ref, done_ref, sem,
):
    _, cells_x, _, _ = u0_ref.shape
    cells_y = done_ref.shape[2]
    lane = lane_ids()
    first = wall_lane()

    def held(x):
        return x + HALO if x < HALO else x - cells_x + HALO + 6

    beyond = [x for p in range(HALO) for x in (p - HALO, cells_x + p)]
    for x in beyond:
        source, p = (xbelow_ref, x + HALO) if x < 0 else (xabove_ref, x - cells_x)
        own = source[3 * HALO + p]
        hs_ref[held(x), WINDOW, :] = own
        for ch in range(3):
            column = column_of(rbf_ref[...], ch, x, cells_x)
            h0_ref[ch, held(x), WINDOW, :] = jnp.where(first & (own > 0.0), column, source[ch * HALO + p])
    for ch in range(4):
        above = roll_lanes(xabove_ref[4 * HALO], -32 * ch)
        below = roll_lanes(xbelow_ref[4 * HALO], -32 * ch)
        side = jnp.where(lane < 8 * HALO, above, jnp.where(lane >= LANES - 8 * HALO, below, 0.0))
        if ch < 3:
            e_ref[0, ch, 0, WINDOW, :] = wide_ref[ch]
            e_ref[0, ch, 1, WINDOW, :] = side
        else:
            eside_ref[WINDOW, :] = side

    def stiff(x):
        return s_ref.at[x] if 0 <= x < cells_x else hs_ref.at[held(x)]

    def field(sweep, ch, x):
        if sweep <= x < cells_x - sweep:
            return (u0_ref, u1_ref, u2_ref)[sweep].at[ch, x]
        return (h0_ref, h1_ref, h2_ref)[sweep].at[ch, held(x)]

    edge_stiff = (es_ref, eside_ref)

    ends = zeros()
    for x in beyond:
        ends = to_edge(ends, stiff(x)[WINDOW, :], spot(x)[1])
    for tile, middle in ((0, cs_ref[...]), (1, ends)):
        others = beside_edge(edge_stiff[tile], edge_stiff[1 - tile][WINDOW, :], middle)
        for k, weight in enumerate(normalised(edge_stiff[tile][WINDOW, :], others)):
            ew_ref[k, tile] = weight
    for x in (-2, -1, 0, cells_x - 1, cells_x, cells_x + 1):
        own = stiff(x)[WINDOW, :]
        tile, g = spot(x)
        down, up = beside(own, from_edge(edge_stiff[tile][WINDOW, :], g))
        others = (
            stiff(x - 1)[WINDOW, :],
            stiff(x + 1)[WINDOW, :],
            stiff(x)[BEFORE, :],
            stiff(x)[AFTER, :],
            down,
            up,
        )
        for k, weight in enumerate(normalised(own, others)):
            hw_ref[k, held(x)] = weight

    for sweep in range(SWEEPS):
        last = sweep == SWEEPS - 1
        planes = [x for p in range(HALO) for x in (sweep - 2 + p, cells_x + 1 - sweep - p)]
        for x in planes:
            tile, g = spot(x)
            if 1 <= x < cells_x - 1:
                weights = [w_ref[k, x] for k in range(6)]
            else:
                weights = [hw_ref[k, held(x)] for k in range(6)]
            for ch in range(3):
                here = field(sweep, ch, x)
                own = here[WINDOW, :]
                down, up = beside(own, from_edge(e_ref[sweep, ch, tile, WINDOW, :], g))
                others = (
                    field(sweep, ch, x - 1)[WINDOW, :],
                    field(sweep, ch, x + 1)[WINDOW, :],
                    here[BEFORE, :],
                    here[AFTER, :],
                    down,
                    up,
                )
                new = jnp.where(first, own, relaxed(own, others, weights))
                if last:
                    done_ref[ch, x if x < HALO else x - cells_x + 2 * HALO] = new[2 : 2 + cells_y]
                else:
                    (h1_ref, h2_ref)[sweep][ch, held(x), WINDOW, :] = new
        if last:
            break
        for ch in range(3):
            if sweep == 0:
                ends = zeros()
                for x in beyond:
                    ends = to_edge(ends, field(0, ch, x)[WINDOW, :], spot(x)[1])
                middles = (c_ref[0, ch], ends)
            else:
                ends = c_ref[1, ch]
                for x in (0, cells_x - 1):
                    ends = to_edge(ends, field(1, ch, x)[WINDOW, :], x)
                middles = (ends,)
            for tile, middle in enumerate(middles):
                others = beside_edge(e_ref.at[sweep, ch, tile], e_ref[sweep, ch, 1 - tile, WINDOW, :], middle)
                weights = [ew_ref[k, tile] for k in range(6)]
                e_ref[sweep + 1, ch, tile, WINDOW, :] = relaxed(
                    e_ref[sweep, ch, tile, WINDOW, :], others, weights
                )
    copies = []
    for ch in range(3):
        for side, x in enumerate((0, cells_x - HALO)):
            copies.append(
                pltpu.make_async_copy(
                    done_ref.at[ch, pl.ds(side * HALO, HALO)],
                    out_ref.at[ch, pl.ds(x, HALO)],
                    sem.at[2 * ch + side],
                )
            )
    for copy in copies:
        copy.start()
    for copy in copies:
        copy.wait()


def step(value, axis, by):
    size = lax.axis_size(axis)
    return lax.ppermute(value, axis, [(i, i + by) for i in range(size) if 0 <= i + by < size])


def body(centre_coef, centre_index, stiff_factor, prev_disp):
    cells_x, cells_y, cells_z = stiff_factor.shape
    count_x = cells_x * lax.axis_size("gx")
    count_y = cells_y * lax.axis_size("gy")
    count_z = cells_z * lax.axis_size("gz")
    blocks = lax.axis_size("gx") * lax.axis_size("gy")
    depth = lax.axis_size("gz")
    scratch = pltpu.VMEM
    num = jnp.float32

    rows_y = 4 * cells_x * HALO
    rows, low, high, ylow, yhigh = kernel_call(
        functools.partial(begin_kernel, float(count_z)),
        "pack_z",
        (
            f32(blocks, LANES),
            f32(2, cells_y, LANES),
            f32(2, cells_y, LANES),
            f32(rows_y, LANES),
            f32(rows_y, LANES),
        ),
        2000 * MEGA,
        (centre_coef.T, centre_index[None]),
        (
            scratch((3, cells_x, cells_y, LANES), num),
            scratch((cells_x, cells_y, LANES), num),
            scratch((4, cells_y, LANES), num),
            pltpu.SemaphoreType.DMA((4,)),
        ),
        far=tuple(pltpu.with_memory_space_constraint(a, pltpu.HBM) for a in (prev_disp, stiff_factor)),
    )
    centres = lax.all_to_all(rows.reshape(blocks, 1, LANES), ("gx", "gy"), 0, 0, tiled=True)
    zabove, zbelow = step(low, "gz", -1), step(high, "gz", 1)

    table = stencil(count_x, count_y, count_z)
    (share,) = kernel_call(
        functools.partial(rbf_kernel, table, cells_x, cells_y, count_y),
        "rbf",
        (f32(depth, HALF, LANES),),
        1500 * MEGA,
        (centres.reshape(blocks, LANES),),
        (scratch((ROWS, LANES), num),),
    )
    shares = lax.all_to_all(share, "gz", 0, 0, tiled=True)

    rows_all = -(-(rows_y + 4 * HALO) // 8) * 8
    edge, ylow, yhigh = kernel_call(
        pack_y_kernel,
        "pack_y",
        (f32(4, cells_y, LANES), f32(rows_all, LANES), f32(rows_all, LANES)),
        300 * MEGA,
        (zabove, zbelow, ylow, yhigh),
        after=(share,),
    )
    yabove, ybelow = step(ylow, "gy", -1), step(yhigh, "gy", 1)

    xlow, xhigh = kernel_call(
        functools.partial(pack_x_kernel, float(count_z)),
        "pack_x",
        (f32(4 * HALO + 1, WIN, LANES), f32(4 * HALO + 1, WIN, LANES)),
        1000 * MEGA,
        (edge, yabove, ybelow),
        (scratch((2, 4, HALO, cells_y, LANES), num), scratch((4, WIN, LANES), num), pltpu.SemaphoreType.DMA((2, 4))),
        far=(prev_disp, stiff_factor),
    )
    xabove, xbelow = step(xlow, "gx", -1), step(xhigh, "gx", 1)

    u0, u1, u2, s, w, es, cs, c, rbf, wide, out = kernel_call(
        functools.partial(inner_kernel, float(count_z)),
        "inner",
        (
            near(3, cells_x, ROWS, LANES),
            near(3, cells_x, ROWS, LANES),
            near(3, cells_x, ROWS, LANES),
            near(cells_x, ROWS, LANES),
            near(6, cells_x, WIN, LANES),
            near(ROWS, LANES),
            near(WIN, LANES),
            near(2, 3, WIN, LANES),
            near(WIN, LANES),
            near(4, WIN, LANES),
            Far((3, cells_x, cells_y, cells_z), num),
        ),
        9000 * MEGA,
        (),
        (
            scratch((3, cells_x, cells_y, LANES), num),
            scratch((cells_x, cells_y, LANES), num),
            scratch((4, cells_y, LANES), num),
            scratch((rows_all, LANES), num),
            scratch((rows_all, LANES), num),
            scratch((depth, HALF, LANES), num),
            scratch((3, 3, ROWS, LANES), num),
            scratch((6, WIN, LANES), num),
            scratch((3, cells_x, cells_y, LANES), num),
            pltpu.SemaphoreType.DMA((9,)),
        ),
        far=(prev_disp, stiff_factor, edge, yabove, ybelow, shares),
    )

    (out,) = kernel_call(
        outer_kernel,
        "outer",
        (Far((3, cells_x, cells_y, cells_z), num),),
        5500 * MEGA,
        (u0, u1, u2, s, w, wide, es, cs, c, rbf, xabove, xbelow),
        (
            scratch((3, 12, ROWS, LANES), num),
            scratch((3, 12, ROWS, LANES), num),
            scratch((3, 12, ROWS, LANES), num),
            scratch((12, ROWS, LANES), num),
            scratch((6, 12, WIN, LANES), num),
            scratch((3, 3, 2, ROWS, LANES), num),
            scratch((ROWS, LANES), num),
            scratch((6, 2, WIN, LANES), num),
            scratch((WIN, LANES), num),
            scratch((3, 2 * HALO, cells_y, LANES), num),
            pltpu.SemaphoreType.DMA((6,)),
        ),
        far=(out,),
        aliases={12: 0},
    )
    return out


def solution(mesh):
    placed = (
        P(("gx", "gy", "gz"), None),
        P(("gx", "gy", "gz")),
        P("gx", "gy", "gz"),
        P(None, "gx", "gy", "gz"),
    )
    return jax.shard_map(
        body, mesh=mesh, in_specs=placed, out_specs=P(None, "gx", "gy", "gz"), check_vma=False
    )
```

```python
import functools
import math

import jax
import jax.numpy as jnp
from jax import lax
from jax.experimental import pallas as pl
from jax.experimental.pallas import tpu as pltpu
from jax.sharding import PartitionSpec as P

SWEEPS = 3
RADIUS = 0.02
OMEGA = 0.8

HALO = 3
TOP = 8
WIN = 72
HALF = 40
ROWS = 88
LANES = 128
MEGA = 1_100_000
VMEM_LIMIT = 16 * 1024 * 1024


def lane_ids(rows=WIN):
    return lax.broadcasted_iota(jnp.int32, (rows, LANES), 1)


def roll_lanes(value, shift):
    if not isinstance(shift, int):
        return pltpu.roll(value, shift % LANES, 1)
    return pltpu.roll(value, shift % LANES, 1) if shift % LANES else value


def kernel_call(kernel, name, outs, flops, args, scratch=(), after=(), far=(), aliases=None):
    moved = sum(math.prod(a.shape) * 4 for a in (*args, *outs))
    anywhere = pl.BlockSpec(memory_space=pl.ANY)
    return pl.pallas_call(
        kernel,
        name=name,
        out_shape=outs,
        in_specs=[pl.BlockSpec(memory_space=pltpu.VMEM)] * len(args) + [anywhere] * (len(far) + len(after)),
        out_specs=tuple(anywhere if isinstance(o, Far) else pl.BlockSpec(memory_space=pltpu.VMEM) for o in outs),
        scratch_shapes=list(scratch),
        input_output_aliases=aliases or {},
        compiler_params=pltpu.CompilerParams(vmem_limit_bytes=VMEM_LIMIT),
        cost_estimate=pl.CostEstimate(flops=flops, bytes_accessed=moved, transcendentals=0),
    )(*args, *far, *after)


class Far(jax.ShapeDtypeStruct):
    pass


def f32(*shape):
    return jax.ShapeDtypeStruct(shape, jnp.float32)


def in_hbm(value):
    return pltpu.with_memory_space_constraint(value, pltpu.HBM)


def near(*shape):
    return pltpu.VMEM(shape, jnp.float32)


def wall_scale(count_z, cells_z):
    deep = (lax.axis_index("gz") * cells_z + lane_ids(1)).astype(jnp.float32) + 0.5
    return count_z / deep


def begin_kernel(
    count_z,
    prev_ref,
    stiff_ref,
    coefs_ref,
    indices_ref,
    rows_ref,
    low_ref,
    high_ref,
    ylow_ref,
    yhigh_ref,
    prevv_ref,
    raw_ref,
    edge_ref,
    coef_ref,
    index_ref,
    sems,
):
    _, cells_x, cells_y, cells_z = prevv_ref.shape
    copies = [pltpu.make_async_copy(prev_ref.at[ch], prevv_ref.at[ch], sems.at[ch]) for ch in range(3)]
    copies.append(pltpu.make_async_copy(stiff_ref, raw_ref, sems.at[3]))
    short = [
        pltpu.make_async_copy(coefs_ref, coef_ref, sems.at[4]),
        pltpu.make_async_copy(indices_ref, index_ref, sems.at[5]),
    ]
    for copy in short + copies:
        copy.start()
    for copy in short:
        copy.wait()
    row = jnp.concatenate(
        [coef_ref[f : f + 1, :] for f in range(3)] + [index_ref[...].astype(jnp.float32)], axis=1
    )
    rows_ref[...] = jnp.broadcast_to(row, rows_ref.shape)
    scale = wall_scale(count_z, cells_z)
    lane = lax.broadcasted_iota(jnp.int32, (8, LANES), 1)
    place = lane % 8
    pick = jnp.where(place <= 3, jnp.clip(3 - place, 0, 2), cells_z - 1 - jnp.clip(place - 4, 0, 2))
    for ch in range(4):
        copies[ch].wait()
        for tile in range(cells_y // 8):
            rows = pl.ds(8 * tile, 8)
            edge = jnp.zeros((8, LANES), jnp.float32)
            for x in range(cells_x):
                if ch < 3:
                    value = prevv_ref[ch, x, rows, :]
                else:
                    value = raw_ref[x, rows, :] * scale
                picked = jnp.take_along_axis(value, pick, axis=1)
                edge = jnp.where(lane // 8 == x, picked, edge)
            edge_ref[ch, rows, :] = edge
        for x in range(cells_x):
            at = pl.ds((ch * cells_x + x) * HALO, HALO)
            plane = prevv_ref.at[ch, x] if ch < 3 else raw_ref.at[x]
            factor = 1.0 if ch < 3 else scale
            ylow_ref[at, :] = plane[:HALO, :] * factor
            yhigh_ref[at, :] = plane[cells_y - HALO :, :] * factor
    place = lane_ids(cells_y) % 8
    for pair in range(2):
        even, odd = edge_ref[2 * pair], edge_ref[2 * pair + 1]
        low_ref[pair] = jnp.where(place <= 3, even, roll_lanes(odd, 3))
        high_ref[pair] = jnp.where(place >= 4, even, roll_lanes(odd, -3))


def pack_y_kernel(above_ref, below_ref, ylow_ref, yhigh_ref, edge_ref, outlow_ref, outhigh_ref):
    rows = above_ref.shape[1]
    place = lane_ids(rows) % 8
    upper = (place >= 1) & (place <= 3)
    lower = (place >= 4) & (place <= 6)
    base = ylow_ref.shape[0]
    outlow_ref[:base, :] = ylow_ref[...]
    outhigh_ref[:base, :] = yhigh_ref[...]
    for ch in range(4):
        above, below = above_ref[ch // 2], below_ref[ch // 2]
        if ch % 2:
            above, below = roll_lanes(above, -3), roll_lanes(below, 3)
        edge = jnp.where(upper, above, jnp.where(lower, below, 0.0))
        edge_ref[ch] = edge
        at = pl.ds(base + ch * HALO, HALO)
        outlow_ref[at, :] = edge[:HALO]
        outhigh_ref[at, :] = edge[rows - HALO :]
    rest = outlow_ref.shape[0] - base - 4 * HALO
    outlow_ref[base + 4 * HALO :, :] = jnp.zeros((rest, LANES), jnp.float32)
    outhigh_ref[base + 4 * HALO :, :] = jnp.zeros((rest, LANES), jnp.float32)


def fill(out, below_ref, middle, above_ref, at):
    cells_y = middle.shape[0]
    out[0:2, :] = below_ref[at + 1 : at + HALO, :]
    out[2 : 2 + cells_y, :] = middle
    out[2 + cells_y : 2 + cells_y + HALO, :] = above_ref[at : at + HALO, :]
    out[2 + cells_y + HALO : WIN, :] = jnp.zeros((WIN - 2 - cells_y - HALO, LANES), jnp.float32)


def pack_x_kernel(
    count_z, edge_ref, yabove_ref, ybelow_ref, prev_ref, stiff_ref, low_ref, high_ref, wide_ref
):
    _, cells_x, cells_y, cells_z = prev_ref.shape
    scale = wall_scale(count_z, cells_z)
    lane = lane_ids()
    base = 4 * cells_x * HALO
    low = jnp.zeros((WIN, LANES), jnp.float32)
    high = low

    for ch in range(4):
        fill(wide_ref.at[ch], ybelow_ref, edge_ref[ch], yabove_ref, base + ch * HALO)
        turned = roll_lanes(wide_ref[ch], 32 * ch)
        at_low = (lane - 32 * ch) & (LANES - 1)
        low = jnp.where(at_low < 8 * HALO, turned, low)
        high = jnp.where(at_low >= LANES - 8 * HALO, turned, high)
    low_ref[4 * HALO] = low
    high_ref[4 * HALO] = high
    for side, out in enumerate((low_ref, high_ref)):
        for ch in range(4):
            for p in range(HALO):
                x = p + side * (cells_x - HALO)
                middle = prev_ref[ch, x] if ch < 3 else stiff_ref[x] * scale
                fill(out.at[ch * HALO + p], ybelow_ref, middle, yabove_ref, (ch * cells_x + x) * HALO)


def stencil(count_x, count_y, count_z):
    table = {}
    for step_x in range(int(RADIUS * count_x) + 2):
        for step_y in range(int(RADIUS * count_y) + 2):
            square = (step_x / count_x) ** 2 + (step_y / count_y) ** 2 + (0.5 / count_z) ** 2
            ratio = math.sqrt(square) / RADIUS
            lead = max(1.0 - ratio, 0.0)
            if lead > 0.0:
                table[step_x, step_y] = lead**4 * (4.0 * ratio + 1.0)
    return table


REACH_X = 8
REACH_Y = 8
GRID_X = 32
GRID_Y = 80


def rbf_kernel(table, cells_x, cells_y, count_y, centres_ref, _, out_ref, grid_ref):
    slots = centres_ref.shape[0] // 4
    first_x = (lax.axis_index("gx") * cells_x - REACH_X).astype(jnp.float32)
    first_y = (lax.axis_index("gy") * cells_y - REACH_Y).astype(jnp.float32)
    quarter = lane_ids(slots) // 32
    fields = []
    for f in range(4):
        field = jnp.zeros((slots, LANES), jnp.float32)
        for k in range(4):
            part = roll_lanes(centres_ref[k * slots : (k + 1) * slots, :], 32 * (k - f))
            field = jnp.where(quarter == k, part, field)
        fields.append(field)
    index = fields[3]
    at_x = jnp.floor(index * (1.0 / count_y))
    at_y = index - at_x * count_y - first_y
    at_x = at_x - first_x
    heads = [f.astype(jnp.bfloat16).astype(jnp.float32) for f in fields[:3]]
    tails = [f - h for f, h in zip(fields[:3], heads)]
    row_y = lax.broadcasted_iota(jnp.int32, (GRID_Y, LANES), 0).astype(jnp.float32)
    row_x = lax.broadcasted_iota(jnp.int32, (GRID_X, LANES), 0).astype(jnp.float32)
    total = jnp.zeros((GRID_Y, 2 * LANES), jnp.float32)
    blank = jnp.zeros((LANES - 3 * GRID_X, LANES), jnp.float32)
    for q in range(0, slots, 2):
        left, right = [], []
        for r in (q, q + 1):
            hit_y = at_y[r : r + 1, :] == row_y
            hit_x = at_x[r : r + 1, :] == row_x
            left.append(jnp.where(hit_y, 1.0, 0.0).astype(jnp.bfloat16))
            pieces = []
            for group in (heads, tails):
                pieces += [jnp.where(hit_x, g[r : r + 1, :], 0.0) for g in group]
                pieces.append(blank)
            right.append(jnp.concatenate(pieces, axis=0).astype(jnp.bfloat16))
        total = total + lax.dot_general(
            jnp.concatenate(left, axis=1),
            jnp.concatenate(right, axis=1),
            (((1,), (1,)), ((), ())),
            preferred_element_type=jnp.float32,
        )
    grid = total[:, :LANES] + total[:, LANES:]
    reach_x = max(a for a, _ in table)
    reach_y = max(b for _, b in table)
    result = jnp.zeros((WIN, LANES), jnp.float32)
    for step_x in range(reach_x + 1):
        value = roll_lanes(grid, 2 - REACH_X + step_x)
        if step_x:
            value = value + roll_lanes(grid, 2 - REACH_X - step_x)
        grid_ref[:GRID_Y, :] = value
        for step_y in range(reach_y + 1):
            phi = table.get((step_x, step_y))
            if phi is None:
                continue
            start = REACH_Y - 2
            part = grid_ref[start + step_y : start + step_y + WIN, :]
            if step_y:
                part = part + grid_ref[start - step_y : start - step_y + WIN, :]
            result = result + phi * part
    lane = lane_ids()
    width = cells_x + 4
    close = jnp.where(
        lane < width,
        result,
        jnp.where(lane < 2 * width, roll_lanes(result, width - 32), roll_lanes(result, 2 * (width - 32))),
    )
    half = out_ref.shape[1]
    share = jnp.where(lane_ids(half) < LANES // 2, close[:half], roll_lanes(close[WIN - half :], LANES // 2))
    for k in range(out_ref.shape[0]):
        out_ref[k] = share


WINDOW = pl.ds(TOP, WIN)
BEFORE = pl.ds(TOP - 1, WIN)
AFTER = pl.ds(TOP + 1, WIN)


def spot(x):
    if isinstance(x, int):
        return (0 if 0 <= x < 16 else 1), x % 16
    return 0, x


def beside(value, edge):
    lane = lane_ids()
    down = jnp.where(lane == 0, edge, roll_lanes(value, 1))
    up = jnp.where(lane == LANES - 1, edge, roll_lanes(value, -1))
    return down, up


def from_edge(tile, g):
    return roll_lanes(tile, LANES - 4 - 8 * g)


def to_edge(old, plane, g):
    lane = lane_ids()
    here = (lane // 8 == g) & ((lane % 8 == 3) | (lane % 8 == 4))
    return jnp.where(here, roll_lanes(plane, 8 * g + 4), old)


def beside_edge(own_ref, other, middle):
    lane = lane_ids()
    place = lane % 8
    own = own_ref[WINDOW, :]
    left = jnp.where(lane >= 8, roll_lanes(own, 8), roll_lanes(other, 8))
    right = jnp.where(lane < LANES - 8, roll_lanes(own, -8), roll_lanes(other, -8))
    minus = jnp.where(place == 4, middle, roll_lanes(own, 1))
    plus = jnp.where(place == 3, middle, roll_lanes(own, -1))
    return left, right, own_ref[BEFORE, :], own_ref[AFTER, :], minus, plus


def normalised(own, others):
    faces = [0.5 * (own + other) for other in others]
    total = functools.reduce(lambda a, b: a + b, faces)
    inside = own > 0.0
    factor = jnp.where(inside, OMEGA / jnp.where(inside, total, 1.0), 0.0)
    return [face * factor for face in faces]


def relaxed(own, others, weights):
    new = (1.0 - OMEGA) * own
    for weight, other in zip(weights, others):
        new = new + weight * other
    return new


def zeros():
    return jnp.zeros((WIN, LANES), jnp.float32)


def wall_lane():
    return (lane_ids() == 0) & (lax.axis_index("gz") == 0)


def column_of(rbf, ch, x, cells_x):
    return roll_lanes(rbf, 2 * LANES - 2 - (cells_x + 4) * ch - x)


def inner_kernel(
    count_z, prev_ref, stiff_ref, edge_ref, yabove_ref, ybelow_ref, shares_ref,
    u0_ref, u1_ref, u2_ref, s_ref, w_ref, es_ref, cs_ref, c_ref, rbf_ref, widev_ref, done_ref,
    e_ref, ew_ref,
):
    _, cells_x, cells_y, cells_z = prev_ref.shape
    first = wall_lane()
    scale = wall_scale(count_z, cells_z)
    main = pl.ds(TOP + 2, cells_y)

    def assemble(ch, x):
        at = (ch * cells_x + x) * HALO
        plane = u0_ref.at[ch, x] if ch < 3 else s_ref.at[x]
        plane[main, :] = prev_ref[ch, x] if ch < 3 else stiff_ref[x] * scale
        plane[TOP - 1 : TOP + 2, :] = ybelow_ref[at : at + HALO, :]
        plane[TOP + 2 + cells_y : TOP + 2 + cells_y + HALO, :] = yabove_ref[at : at + HALO, :]

    for x in range(cells_x):
        assemble(3, x)
    for ch in range(4):
        fill(widev_ref.at[ch], ybelow_ref, edge_ref[ch], yabove_ref, (4 * cells_x + ch) * HALO)
    es_ref[WINDOW, :] = widev_ref[3]
    cs_ref[...] = zeros()
    for x in (0, cells_x - 1):
        cs_ref[...] = to_edge(cs_ref[...], s_ref[x, WINDOW, :], x)

    def weigh(x, carry):
        own = s_ref[x, WINDOW, :]
        down, up = beside(own, from_edge(es_ref[WINDOW, :], x))
        others = (s_ref[x - 1, WINDOW, :], s_ref[x + 1, WINDOW, :], s_ref[x, BEFORE, :], s_ref[x, AFTER, :], down, up)
        for k, weight in enumerate(normalised(own, others)):
            w_ref[k, x] = weight
        cs_ref[...] = to_edge(cs_ref[...], own, x)
        return carry

    lax.fori_loop(1, cells_x - 1, weigh, 0, unroll=14)
    others = beside_edge(es_ref, zeros(), cs_ref[...])
    for k, weight in enumerate(normalised(es_ref[WINDOW, :], others)):
        ew_ref[k] = weight

    for ch in range(3):
        e_ref[0, ch, WINDOW, :] = widev_ref[ch]
        for x in range(cells_x):
            assemble(ch, x)
    rbf_ref[...] = zeros()

    @pl.when(lax.axis_index("gz") == 0)
    def _():
        share = shares_ref[0]
        for k in range(1, shares_ref.shape[0]):
            share = share + shares_ref[k]
        half = share.shape[0]
        rbf_ref[WIN - half :, :] = roll_lanes(share, LANES // 2)
        rbf_ref[:half, :] = share
        rbf = rbf_ref[...]

        def layer(x, carry):
            own = first & (s_ref[x, WINDOW, :] > 0.0)
            for ch in range(3):
                column = column_of(rbf, ch, x, cells_x)
                u0_ref[ch, x, WINDOW, :] = jnp.where(own, column, u0_ref[ch, x, WINDOW, :])
            return carry

        lax.fori_loop(0, cells_x, layer, 0, unroll=16)

    for ch in range(3):
        ends = zeros()
        for x in range(cells_x):
            ends = to_edge(ends, u0_ref[ch, x, WINDOW, :], x)
        c_ref[0, ch] = ends
        c_ref[1, ch] = zeros()

    stages = (u0_ref, u1_ref, u2_ref)
    for sweep in range(SWEEPS):
        now, last = stages[sweep], sweep == SWEEPS - 1

        def relax(x, carry):
            weights = [w_ref[k, x] for k in range(6)]
            for ch in range(3):
                own = now[ch, x, WINDOW, :]
                down, up = beside(own, from_edge(e_ref[sweep, ch, WINDOW, :], x))
                others = (
                    now[ch, x - 1, WINDOW, :],
                    now[ch, x + 1, WINDOW, :],
                    now[ch, x, BEFORE, :],
                    now[ch, x, AFTER, :],
                    down,
                    up,
                )
                new = jnp.where(first, own, relaxed(own, others, weights))
                if last:
                    done_ref[ch, x] = new[2 : 2 + cells_y]
                else:
                    stages[sweep + 1][ch, x, WINDOW, :] = new
                if sweep == 0:
                    c_ref[1, ch] = to_edge(c_ref[1, ch], new, x)
            return carry

        lax.fori_loop(1 + sweep, cells_x - 1 - sweep, relax, 0, unroll=(14, 12, 10)[sweep])
        if not last:
            for ch in range(3):
                others = beside_edge(e_ref.at[sweep, ch], zeros(), c_ref[sweep, ch])
                weights = [ew_ref[k] for k in range(6)]
                e_ref[sweep + 1, ch, WINDOW, :] = relaxed(e_ref[sweep, ch, WINDOW, :], others, weights)


def outer_kernel(
    u0_ref, u1_ref, u2_ref, s_ref, w_ref, wide_ref, es_ref, cs_ref, c_ref, rbf_ref, done_ref, xabove_ref, xbelow_ref,
    out_ref,
    h0_ref, h1_ref, h2_ref, hs_ref, hw_ref, e_ref, eside_ref, ew_ref, new_ref, sems,
):
    _, cells_x, _, _ = u0_ref.shape
    cells_y = done_ref.shape[2]
    lane = lane_ids()
    first = wall_lane()
    inside = pl.ds(HALO, cells_x - 2 * HALO)
    copies = [pltpu.make_async_copy(done_ref.at[ch, inside], out_ref.at[ch, inside], sems.at[ch]) for ch in range(3)]
    for copy in copies:
        copy.start()

    def held(x):
        return x + HALO if x < HALO else x - cells_x + HALO + 6

    beyond = [x for p in range(HALO) for x in (p - HALO, cells_x + p)]
    for x in beyond:
        source, p = (xbelow_ref, x + HALO) if x < 0 else (xabove_ref, x - cells_x)
        own = source[3 * HALO + p]
        hs_ref[held(x), WINDOW, :] = own
        for ch in range(3):
            column = column_of(rbf_ref[...], ch, x, cells_x)
            h0_ref[ch, held(x), WINDOW, :] = jnp.where(first & (own > 0.0), column, source[ch * HALO + p])
    for ch in range(4):
        above = roll_lanes(xabove_ref[4 * HALO], -32 * ch)
        below = roll_lanes(xbelow_ref[4 * HALO], -32 * ch)
        side = jnp.where(lane < 8 * HALO, above, jnp.where(lane >= LANES - 8 * HALO, below, 0.0))
        if ch < 3:
            e_ref[0, ch, 0, WINDOW, :] = wide_ref[ch]
            e_ref[0, ch, 1, WINDOW, :] = side
        else:
            eside_ref[WINDOW, :] = side

    def stiff(x):
        return s_ref.at[x] if 0 <= x < cells_x else hs_ref.at[held(x)]

    def field(sweep, ch, x):
        if sweep <= x < cells_x - sweep:
            return (u0_ref, u1_ref, u2_ref)[sweep].at[ch, x]
        return (h0_ref, h1_ref, h2_ref)[sweep].at[ch, held(x)]

    edge_stiff = (es_ref, eside_ref)

    ends = zeros()
    for x in beyond:
        ends = to_edge(ends, stiff(x)[WINDOW, :], spot(x)[1])
    for tile, middle in ((0, cs_ref[...]), (1, ends)):
        others = beside_edge(edge_stiff[tile], edge_stiff[1 - tile][WINDOW, :], middle)
        for k, weight in enumerate(normalised(edge_stiff[tile][WINDOW, :], others)):
            ew_ref[k, tile] = weight
    for x in (-2, -1, 0, cells_x - 1, cells_x, cells_x + 1):
        own = stiff(x)[WINDOW, :]
        tile, g = spot(x)
        down, up = beside(own, from_edge(edge_stiff[tile][WINDOW, :], g))
        others = (
            stiff(x - 1)[WINDOW, :],
            stiff(x + 1)[WINDOW, :],
            stiff(x)[BEFORE, :],
            stiff(x)[AFTER, :],
            down,
            up,
        )
        for k, weight in enumerate(normalised(own, others)):
            hw_ref[k, held(x)] = weight

    for sweep in range(SWEEPS):
        last = sweep == SWEEPS - 1
        planes = [x for p in range(HALO) for x in (sweep - 2 + p, cells_x + 1 - sweep - p)]
        for x in planes:
            tile, g = spot(x)
            if 1 <= x < cells_x - 1:
                weights = [w_ref[k, x] for k in range(6)]
            else:
                weights = [hw_ref[k, held(x)] for k in range(6)]
            for ch in range(3):
                here = field(sweep, ch, x)
                own = here[WINDOW, :]
                down, up = beside(own, from_edge(e_ref[sweep, ch, tile, WINDOW, :], g))
                others = (
                    field(sweep, ch, x - 1)[WINDOW, :],
                    field(sweep, ch, x + 1)[WINDOW, :],
                    here[BEFORE, :],
                    here[AFTER, :],
                    down,
                    up,
                )
                new = jnp.where(first, own, relaxed(own, others, weights))
                if last:
                    place = x if x < HALO else x - cells_x + 2 * HALO
                    new_ref[ch, place] = new[2 : 2 + cells_y]
                    sem = sems.at[3 + 6 * ch + place]
                    copies.append(pltpu.make_async_copy(new_ref.at[ch, place], out_ref.at[ch, x], sem))
                    copies[-1].start()
                else:
                    (h1_ref, h2_ref)[sweep][ch, held(x), WINDOW, :] = new
        if last:
            break
        for ch in range(3):
            if sweep == 0:
                ends = zeros()
                for x in beyond:
                    ends = to_edge(ends, field(0, ch, x)[WINDOW, :], spot(x)[1])
                middles = (c_ref[0, ch], ends)
            else:
                ends = c_ref[1, ch]
                for x in (0, cells_x - 1):
                    ends = to_edge(ends, field(1, ch, x)[WINDOW, :], x)
                middles = (ends,)
            for tile, middle in enumerate(middles):
                others = beside_edge(e_ref.at[sweep, ch, tile], e_ref[sweep, ch, 1 - tile, WINDOW, :], middle)
                weights = [ew_ref[k, tile] for k in range(6)]
                e_ref[sweep + 1, ch, tile, WINDOW, :] = relaxed(
                    e_ref[sweep, ch, tile, WINDOW, :], others, weights
                )
    for copy in copies:
        copy.wait()


def step(value, axis, by):
    size = lax.axis_size(axis)
    return lax.ppermute(value, axis, [(i, i + by) for i in range(size) if 0 <= i + by < size])


def body(centre_coef, centre_index, stiff_factor, prev_disp):
    cells_x, cells_y, cells_z = stiff_factor.shape
    count_x = cells_x * lax.axis_size("gx")
    count_y = cells_y * lax.axis_size("gy")
    count_z = cells_z * lax.axis_size("gz")
    blocks = lax.axis_size("gx") * lax.axis_size("gy")
    depth = lax.axis_size("gz")
    scratch = pltpu.VMEM
    num = jnp.float32

    rows_y = 4 * cells_x * HALO
    rows, low, high, ylow, yhigh = kernel_call(
        functools.partial(begin_kernel, float(count_z)),
        "pack_z",
        (
            f32(blocks, LANES),
            f32(2, cells_y, LANES),
            f32(2, cells_y, LANES),
            f32(rows_y, LANES),
            f32(rows_y, LANES),
        ),
        2000 * MEGA,
        (),
        (
            scratch((3, cells_x, cells_y, LANES), num),
            scratch((cells_x, cells_y, LANES), num),
            scratch((4, cells_y, LANES), num),
            scratch((3, centre_index.shape[0]), num),
            scratch((1, centre_index.shape[0]), jnp.int32),
            pltpu.SemaphoreType.DMA((6,)),
        ),
        far=tuple(in_hbm(a) for a in (prev_disp, stiff_factor, centre_coef.T, centre_index[None])),
    )
    centres = lax.all_to_all(rows.reshape(blocks, 1, LANES), ("gx", "gy"), 0, 0, tiled=True)
    zabove, zbelow = step(low, "gz", -1), step(high, "gz", 1)

    rows_all = -(-(rows_y + 4 * HALO) // 8) * 8
    edge, ylow, yhigh = kernel_call(
        pack_y_kernel,
        "pack_y",
        (f32(4, cells_y, LANES), f32(rows_all, LANES), f32(rows_all, LANES)),
        300 * MEGA,
        (zabove, zbelow, ylow, yhigh),
    )
    yabove, ybelow = step(ylow, "gy", -1), step(yhigh, "gy", 1)

    table = stencil(count_x, count_y, count_z)
    (share,) = kernel_call(
        functools.partial(rbf_kernel, table, cells_x, cells_y, count_y),
        "rbf",
        (f32(depth, HALF, LANES),),
        1500 * MEGA,
        (centres.reshape(blocks, LANES),),
        (scratch((ROWS, LANES), num),),
        after=(ylow,),
    )
    shares = lax.all_to_all(share, "gz", 0, 0, tiled=True)

    xlow, xhigh = kernel_call(
        functools.partial(pack_x_kernel, float(count_z)),
        "pack_x",
        (f32(4 * HALO + 1, WIN, LANES), f32(4 * HALO + 1, WIN, LANES)),
        8000 * MEGA,
        (edge, yabove, ybelow, prev_disp, stiff_factor),
        (scratch((4, WIN, LANES), num),),
    )
    xabove, xbelow = step(xlow, "gx", -1), step(xhigh, "gx", 1)

    u0, u1, u2, s, w, es, cs, c, rbf, wide, done = kernel_call(
        functools.partial(inner_kernel, float(count_z)),
        "inner",
        (
            near(3, cells_x, ROWS, LANES),
            near(3, cells_x, ROWS, LANES),
            near(3, cells_x, ROWS, LANES),
            near(cells_x, ROWS, LANES),
            near(6, cells_x, WIN, LANES),
            near(ROWS, LANES),
            near(WIN, LANES),
            near(2, 3, WIN, LANES),
            near(WIN, LANES),
            near(4, WIN, LANES),
            near(3, cells_x, cells_y, cells_z),
        ),
        9000 * MEGA,
        (prev_disp, stiff_factor, in_hbm(edge), yabove, ybelow, shares),
        (
            scratch((3, 3, ROWS, LANES), num),
            scratch((6, WIN, LANES), num),
        ),
    )

    (out,) = kernel_call(
        outer_kernel,
        "outer",
        (Far((3, cells_x, cells_y, cells_z), num),),
        5500 * MEGA,
        (u0, u1, u2, s, w, wide, es, cs, c, rbf, done, xabove, xbelow),
        (
            scratch((3, 12, ROWS, LANES), num),
            scratch((3, 12, ROWS, LANES), num),
            scratch((3, 12, ROWS, LANES), num),
            scratch((12, ROWS, LANES), num),
            scratch((6, 12, WIN, LANES), num),
            scratch((3, 3, 2, ROWS, LANES), num),
            scratch((ROWS, LANES), num),
            scratch((6, 2, WIN, LANES), num),
            scratch((3, 2 * HALO, cells_y, LANES), num),
            pltpu.SemaphoreType.DMA((21,)),
        ),
    )
    return out


def solution(mesh):
    placed = (
        P(("gx", "gy", "gz"), None),
        P(("gx", "gy", "gz")),
        P("gx", "gy", "gz"),
        P(None, "gx", "gy", "gz"),
    )
    return jax.shard_map(
        body, mesh=mesh, in_specs=placed, out_specs=P(None, "gx", "gy", "gz"), check_vma=False
    )
```

```python
import functools
import math

import jax
import jax.numpy as jnp
from jax import lax
from jax.experimental import pallas as pl
from jax.experimental.pallas import tpu as pltpu
from jax.sharding import PartitionSpec as P

SWEEPS = 3
RADIUS = 0.02
OMEGA = 0.8

HALO = 3
TOP = 8
WIN = 72
HALF = 40
ROWS = 88
LANES = 128
MEGA = 1_100_000
VMEM_LIMIT = 16 * 1024 * 1024


def lane_ids(rows=WIN):
    return lax.broadcasted_iota(jnp.int32, (rows, LANES), 1)


def roll_lanes(value, shift):
    if not isinstance(shift, int):
        return pltpu.roll(value, shift % LANES, 1)
    return pltpu.roll(value, shift % LANES, 1) if shift % LANES else value


def kernel_call(kernel, name, outs, flops, args, scratch=(), after=(), far=(), aliases=None):
    moved = sum(math.prod(a.shape) * 4 for a in (*args, *outs))
    anywhere = pl.BlockSpec(memory_space=pl.ANY)
    return pl.pallas_call(
        kernel,
        name=name,
        out_shape=outs,
        in_specs=[pl.BlockSpec(memory_space=pltpu.VMEM)] * len(args) + [anywhere] * (len(far) + len(after)),
        out_specs=tuple(anywhere if isinstance(o, Far) else pl.BlockSpec(memory_space=pltpu.VMEM) for o in outs),
        scratch_shapes=list(scratch),
        input_output_aliases=aliases or {},
        compiler_params=pltpu.CompilerParams(vmem_limit_bytes=VMEM_LIMIT),
        cost_estimate=pl.CostEstimate(flops=flops, bytes_accessed=moved, transcendentals=0),
    )(*args, *far, *after)


class Far(jax.ShapeDtypeStruct):
    pass


def f32(*shape):
    return jax.ShapeDtypeStruct(shape, jnp.float32)


def in_hbm(value):
    return pltpu.with_memory_space_constraint(value, pltpu.HBM)


def near(*shape):
    return pltpu.VMEM(shape, jnp.float32)


def wall_scale(count_z, cells_z):
    deep = (lax.axis_index("gz") * cells_z + lane_ids(1)).astype(jnp.float32) + 0.5
    return count_z / deep


def begin_kernel(
    count_z,
    prev_ref,
    stiff_ref,
    coefs_ref,
    indices_ref,
    rows_ref,
    low_ref,
    high_ref,
    ylow_ref,
    yhigh_ref,
    prevv_ref,
    raw_ref,
    edge_ref,
    coef_ref,
    index_ref,
    sems,
):
    _, cells_x, cells_y, cells_z = prevv_ref.shape
    copies = [pltpu.make_async_copy(prev_ref.at[ch], prevv_ref.at[ch], sems.at[ch]) for ch in range(3)]
    copies.append(pltpu.make_async_copy(stiff_ref, raw_ref, sems.at[3]))
    short = [
        pltpu.make_async_copy(coefs_ref, coef_ref, sems.at[4]),
        pltpu.make_async_copy(indices_ref, index_ref, sems.at[5]),
    ]
    for copy in short + copies:
        copy.start()
    for copy in short:
        copy.wait()
    row = jnp.concatenate(
        [coef_ref[f : f + 1, :] for f in range(3)] + [index_ref[...].astype(jnp.float32)], axis=1
    )
    rows_ref[...] = jnp.broadcast_to(row, rows_ref.shape)
    scale = wall_scale(count_z, cells_z)
    lane = lax.broadcasted_iota(jnp.int32, (8, LANES), 1)
    place = lane % 8
    pick = jnp.where(place <= 3, jnp.clip(3 - place, 0, 2), cells_z - 1 - jnp.clip(place - 4, 0, 2))
    for ch in range(4):
        copies[ch].wait()
        for tile in range(cells_y // 8):
            rows = pl.ds(8 * tile, 8)
            edge = jnp.zeros((8, LANES), jnp.float32)
            for x in range(cells_x):
                if ch < 3:
                    value = prevv_ref[ch, x, rows, :]
                else:
                    value = raw_ref[x, rows, :] * scale
                picked = jnp.take_along_axis(value, pick, axis=1)
                edge = jnp.where(lane // 8 == x, picked, edge)
            edge_ref[ch, rows, :] = edge
        for x in range(cells_x):
            at = pl.ds((ch * cells_x + x) * HALO, HALO)
            plane = prevv_ref.at[ch, x] if ch < 3 else raw_ref.at[x]
            factor = 1.0 if ch < 3 else scale
            ylow_ref[at, :] = plane[:HALO, :] * factor
            yhigh_ref[at, :] = plane[cells_y - HALO :, :] * factor
    place = lane_ids(cells_y) % 8
    for pair in range(2):
        even, odd = edge_ref[2 * pair], edge_ref[2 * pair + 1]
        low_ref[pair] = jnp.where(place <= 3, even, roll_lanes(odd, 3))
        high_ref[pair] = jnp.where(place >= 4, even, roll_lanes(odd, -3))


def pack_y_kernel(above_ref, below_ref, ylow_ref, yhigh_ref, edge_ref, outlow_ref, outhigh_ref):
    rows = above_ref.shape[1]
    place = lane_ids(rows) % 8
    upper = (place >= 1) & (place <= 3)
    lower = (place >= 4) & (place <= 6)
    base = ylow_ref.shape[0]
    outlow_ref[:base, :] = ylow_ref[...]
    outhigh_ref[:base, :] = yhigh_ref[...]
    for ch in range(4):
        above, below = above_ref[ch // 2], below_ref[ch // 2]
        if ch % 2:
            above, below = roll_lanes(above, -3), roll_lanes(below, 3)
        edge = jnp.where(upper, above, jnp.where(lower, below, 0.0))
        edge_ref[ch] = edge
        at = pl.ds(base + ch * HALO, HALO)
        outlow_ref[at, :] = edge[:HALO]
        outhigh_ref[at, :] = edge[rows - HALO :]
    rest = outlow_ref.shape[0] - base - 4 * HALO
    outlow_ref[base + 4 * HALO :, :] = jnp.zeros((rest, LANES), jnp.float32)
    outhigh_ref[base + 4 * HALO :, :] = jnp.zeros((rest, LANES), jnp.float32)


def fill(out, below_ref, middle, above_ref, at):
    cells_y = middle.shape[0]
    out[0:2, :] = below_ref[at + 1 : at + HALO, :]
    out[2 : 2 + cells_y, :] = middle
    out[2 + cells_y : 2 + cells_y + HALO, :] = above_ref[at : at + HALO, :]
    out[2 + cells_y + HALO : WIN, :] = jnp.zeros((WIN - 2 - cells_y - HALO, LANES), jnp.float32)


def pack_x_kernel(
    count_z, edge_ref, yabove_ref, ybelow_ref, prev_ref, stiff_ref, low_ref, high_ref, wide_ref
):
    _, cells_x, cells_y, cells_z = prev_ref.shape
    scale = wall_scale(count_z, cells_z)
    lane = lane_ids()
    base = 4 * cells_x * HALO
    low = jnp.zeros((WIN, LANES), jnp.float32)
    high = low

    for ch in range(4):
        fill(wide_ref.at[ch], ybelow_ref, edge_ref[ch], yabove_ref, base + ch * HALO)
        turned = roll_lanes(wide_ref[ch], 32 * ch)
        at_low = (lane - 32 * ch) & (LANES - 1)
        low = jnp.where(at_low < 8 * HALO, turned, low)
        high = jnp.where(at_low >= LANES - 8 * HALO, turned, high)
    low_ref[4 * HALO] = low
    high_ref[4 * HALO] = high
    for side, out in enumerate((low_ref, high_ref)):
        for ch in range(4):
            for p in range(HALO):
                x = p + side * (cells_x - HALO)
                middle = prev_ref[ch, x] if ch < 3 else stiff_ref[x] * scale
                fill(out.at[ch * HALO + p], ybelow_ref, middle, yabove_ref, (ch * cells_x + x) * HALO)


def stencil(count_x, count_y, count_z):
    table = {}
    for step_x in range(int(RADIUS * count_x) + 2):
        for step_y in range(int(RADIUS * count_y) + 2):
            square = (step_x / count_x) ** 2 + (step_y / count_y) ** 2 + (0.5 / count_z) ** 2
            ratio = math.sqrt(square) / RADIUS
            lead = max(1.0 - ratio, 0.0)
            if lead > 0.0:
                table[step_x, step_y] = lead**4 * (4.0 * ratio + 1.0)
    return table


REACH_X = 8
REACH_Y = 8
GRID_X = 32
GRID_Y = 80


def rbf_kernel(table, cells_x, cells_y, count_y, centres_ref, _, out_ref, grid_ref):
    slots = centres_ref.shape[0] // 4
    first_x = (lax.axis_index("gx") * cells_x - REACH_X).astype(jnp.float32)
    first_y = (lax.axis_index("gy") * cells_y - REACH_Y).astype(jnp.float32)
    quarter = lane_ids(slots) // 32
    fields = []
    for f in range(4):
        field = jnp.zeros((slots, LANES), jnp.float32)
        for k in range(4):
            part = roll_lanes(centres_ref[k * slots : (k + 1) * slots, :], 32 * (k - f))
            field = jnp.where(quarter == k, part, field)
        fields.append(field)
    index = fields[3]
    at_x = jnp.floor(index * (1.0 / count_y))
    at_y = index - at_x * count_y - first_y
    at_x = at_x - first_x
    heads = [f.astype(jnp.bfloat16).astype(jnp.float32) for f in fields[:3]]
    tails = [f - h for f, h in zip(fields[:3], heads)]
    row_y = lax.broadcasted_iota(jnp.int32, (GRID_Y, LANES), 0).astype(jnp.float32)
    row_x = lax.broadcasted_iota(jnp.int32, (GRID_X, LANES), 0).astype(jnp.float32)
    total = jnp.zeros((GRID_Y, 2 * LANES), jnp.float32)
    blank = jnp.zeros((LANES - 3 * GRID_X, LANES), jnp.float32)
    for q in range(0, slots, 2):
        left, right = [], []
        for r in (q, q + 1):
            hit_y = at_y[r : r + 1, :] == row_y
            hit_x = at_x[r : r + 1, :] == row_x
            left.append(jnp.where(hit_y, 1.0, 0.0).astype(jnp.bfloat16))
            pieces = []
            for group in (heads, tails):
                pieces += [jnp.where(hit_x, g[r : r + 1, :], 0.0) for g in group]
                pieces.append(blank)
            right.append(jnp.concatenate(pieces, axis=0).astype(jnp.bfloat16))
        total = total + lax.dot_general(
            jnp.concatenate(left, axis=1),
            jnp.concatenate(right, axis=1),
            (((1,), (1,)), ((), ())),
            preferred_element_type=jnp.float32,
        )
    grid = total[:, :LANES] + total[:, LANES:]
    reach_x = max(a for a, _ in table)
    reach_y = max(b for _, b in table)
    result = jnp.zeros((WIN, LANES), jnp.float32)
    for step_x in range(reach_x + 1):
        value = roll_lanes(grid, 2 - REACH_X + step_x)
        if step_x:
            value = value + roll_lanes(grid, 2 - REACH_X - step_x)
        grid_ref[:GRID_Y, :] = value
        for step_y in range(reach_y + 1):
            phi = table.get((step_x, step_y))
            if phi is None:
                continue
            start = REACH_Y - 2
            part = grid_ref[start + step_y : start + step_y + WIN, :]
            if step_y:
                part = part + grid_ref[start - step_y : start - step_y + WIN, :]
            result = result + phi * part
    lane = lane_ids()
    width = cells_x + 4
    close = jnp.where(
        lane < width,
        result,
        jnp.where(lane < 2 * width, roll_lanes(result, width - 32), roll_lanes(result, 2 * (width - 32))),
    )
    half = out_ref.shape[1]
    share = jnp.where(lane_ids(half) < LANES // 2, close[:half], roll_lanes(close[WIN - half :], LANES // 2))
    for k in range(out_ref.shape[0]):
        out_ref[k] = share


WINDOW = pl.ds(TOP, WIN)
BEFORE = pl.ds(TOP - 1, WIN)
AFTER = pl.ds(TOP + 1, WIN)


def spot(x):
    if isinstance(x, int):
        return (0 if 0 <= x < 16 else 1), x % 16
    return 0, x


def beside(value, edge):
    lane = lane_ids()
    down = jnp.where(lane == 0, edge, roll_lanes(value, 1))
    up = jnp.where(lane == LANES - 1, edge, roll_lanes(value, -1))
    return down, up


def from_edge(tile, g):
    return roll_lanes(tile, LANES - 4 - 8 * g)


def to_edge(old, plane, g):
    lane = lane_ids()
    here = (lane // 8 == g) & ((lane % 8 == 3) | (lane % 8 == 4))
    return jnp.where(here, roll_lanes(plane, 8 * g + 4), old)


def beside_edge(own_ref, other, middle):
    lane = lane_ids()
    place = lane % 8
    own = own_ref[WINDOW, :]
    left = jnp.where(lane >= 8, roll_lanes(own, 8), roll_lanes(other, 8))
    right = jnp.where(lane < LANES - 8, roll_lanes(own, -8), roll_lanes(other, -8))
    minus = jnp.where(place == 4, middle, roll_lanes(own, 1))
    plus = jnp.where(place == 3, middle, roll_lanes(own, -1))
    return left, right, own_ref[BEFORE, :], own_ref[AFTER, :], minus, plus


def normalised(own, others):
    faces = [0.5 * (own + other) for other in others]
    total = functools.reduce(lambda a, b: a + b, faces)
    inside = own > 0.0
    factor = jnp.where(inside, OMEGA / jnp.where(inside, total, 1.0), 0.0)
    return [face * factor for face in faces]


def relaxed(own, others, weights):
    new = (1.0 - OMEGA) * own
    for weight, other in zip(weights, others):
        new = new + weight * other
    return new


def zeros():
    return jnp.zeros((WIN, LANES), jnp.float32)


def wall_lane():
    return (lane_ids() == 0) & (lax.axis_index("gz") == 0)


def column_of(rbf, ch, x, cells_x):
    return roll_lanes(rbf, 2 * LANES - 2 - (cells_x + 4) * ch - x)


def inner_kernel(
    count_z, prev_ref, stiff_ref, edge_ref, yabove_ref, ybelow_ref, shares_ref,
    u0_ref, u1_ref, u2_ref, s_ref, w_ref, es_ref, cs_ref, c_ref, rbf_ref, widev_ref, done_ref,
    e_ref, ew_ref,
):
    _, cells_x, cells_y, cells_z = prev_ref.shape
    first = wall_lane()
    scale = wall_scale(count_z, cells_z)
    main = pl.ds(TOP + 2, cells_y)

    def assemble(ch, x):
        at = (ch * cells_x + x) * HALO
        plane = u0_ref.at[ch, x] if ch < 3 else s_ref.at[x]
        plane[main, :] = prev_ref[ch, x] if ch < 3 else stiff_ref[x] * scale
        plane[TOP - 1 : TOP + 2, :] = ybelow_ref[at : at + HALO, :]
        plane[TOP + 2 + cells_y : TOP + 2 + cells_y + HALO, :] = yabove_ref[at : at + HALO, :]

    for x in range(cells_x):
        assemble(3, x)
    for ch in range(4):
        fill(widev_ref.at[ch], ybelow_ref, edge_ref[ch], yabove_ref, (4 * cells_x + ch) * HALO)
    es_ref[WINDOW, :] = widev_ref[3]
    ends = zeros()
    for x in range(cells_x):
        ends = to_edge(ends, s_ref[x, WINDOW, :], x)
    cs_ref[...] = ends

    def weigh(x, carry):
        own = s_ref[x, WINDOW, :]
        down, up = beside(own, from_edge(es_ref[WINDOW, :], x))
        others = (s_ref[x - 1, WINDOW, :], s_ref[x + 1, WINDOW, :], s_ref[x, BEFORE, :], s_ref[x, AFTER, :], down, up)
        for k, weight in enumerate(normalised(own, others)):
            w_ref[k, x] = weight
        return carry

    for x in range(1, cells_x - 1):
        weigh(x, 0)
    others = beside_edge(es_ref, zeros(), cs_ref[...])
    for k, weight in enumerate(normalised(es_ref[WINDOW, :], others)):
        ew_ref[k] = weight

    for ch in range(3):
        e_ref[0, ch, WINDOW, :] = widev_ref[ch]
        for x in range(cells_x):
            assemble(ch, x)
    rbf_ref[...] = zeros()

    @pl.when(lax.axis_index("gz") == 0)
    def _():
        share = shares_ref[0]
        for k in range(1, shares_ref.shape[0]):
            share = share + shares_ref[k]
        half = share.shape[0]
        rbf_ref[WIN - half :, :] = roll_lanes(share, LANES // 2)
        rbf_ref[:half, :] = share
        rbf = rbf_ref[...]

        def layer(x, carry):
            own = first & (s_ref[x, WINDOW, :] > 0.0)
            for ch in range(3):
                column = column_of(rbf, ch, x, cells_x)
                u0_ref[ch, x, WINDOW, :] = jnp.where(own, column, u0_ref[ch, x, WINDOW, :])
            return carry

        for x in range(cells_x):
            layer(x, 0)

    stages = (u0_ref, u1_ref, u2_ref)
    for sweep in range(SWEEPS):
        now, last = stages[sweep], sweep == SWEEPS - 1

        def relax(x, carry):
            weights = [w_ref[k, x] for k in range(6)]
            for ch in range(3):
                own = now[ch, x, WINDOW, :]
                down, up = beside(own, from_edge(e_ref[sweep, ch, WINDOW, :], x))
                others = (
                    now[ch, x - 1, WINDOW, :],
                    now[ch, x + 1, WINDOW, :],
                    now[ch, x, BEFORE, :],
                    now[ch, x, AFTER, :],
                    down,
                    up,
                )
                new = jnp.where(first, own, relaxed(own, others, weights))
                if last:
                    done_ref[ch, x] = new[2 : 2 + cells_y]
                else:
                    stages[sweep + 1][ch, x, WINDOW, :] = new
            return carry

        for x in range(1 + sweep, cells_x - 1 - sweep):
            relax(x, 0)
        if not last:
            for ch in range(3):
                ends = zeros()
                for x in range(sweep, cells_x - sweep):
                    ends = to_edge(ends, now[ch, x, WINDOW, :], x)
                c_ref[sweep, ch] = ends
                others = beside_edge(e_ref.at[sweep, ch], zeros(), ends)
                weights = [ew_ref[k] for k in range(6)]
                e_ref[sweep + 1, ch, WINDOW, :] = relaxed(e_ref[sweep, ch, WINDOW, :], others, weights)


def outer_kernel(
    u0_ref, u1_ref, u2_ref, s_ref, w_ref, wide_ref, es_ref, cs_ref, c_ref, rbf_ref, done_ref, xabove_ref, xbelow_ref,
    out_ref,
    h0_ref, h1_ref, h2_ref, hs_ref, hw_ref, e_ref, eside_ref, ew_ref, new_ref, sems,
):
    _, cells_x, _, _ = u0_ref.shape
    cells_y = done_ref.shape[2]
    lane = lane_ids()
    first = wall_lane()
    inside = pl.ds(HALO, cells_x - 2 * HALO)
    copies = [pltpu.make_async_copy(done_ref.at[ch, inside], out_ref.at[ch, inside], sems.at[ch]) for ch in range(3)]
    for copy in copies:
        copy.start()

    def held(x):
        return x + HALO if x < HALO else x - cells_x + HALO + 6

    beyond = [x for p in range(HALO) for x in (p - HALO, cells_x + p)]
    for x in beyond:
        source, p = (xbelow_ref, x + HALO) if x < 0 else (xabove_ref, x - cells_x)
        own = source[3 * HALO + p]
        hs_ref[held(x), WINDOW, :] = own
        for ch in range(3):
            column = column_of(rbf_ref[...], ch, x, cells_x)
            h0_ref[ch, held(x), WINDOW, :] = jnp.where(first & (own > 0.0), column, source[ch * HALO + p])
    for ch in range(4):
        above = roll_lanes(xabove_ref[4 * HALO], -32 * ch)
        below = roll_lanes(xbelow_ref[4 * HALO], -32 * ch)
        side = jnp.where(lane < 8 * HALO, above, jnp.where(lane >= LANES - 8 * HALO, below, 0.0))
        if ch < 3:
            e_ref[0, ch, 0, WINDOW, :] = wide_ref[ch]
            e_ref[0, ch, 1, WINDOW, :] = side
        else:
            eside_ref[WINDOW, :] = side

    def stiff(x):
        return s_ref.at[x] if 0 <= x < cells_x else hs_ref.at[held(x)]

    def field(sweep, ch, x):
        if sweep <= x < cells_x - sweep:
            return (u0_ref, u1_ref, u2_ref)[sweep].at[ch, x]
        return (h0_ref, h1_ref, h2_ref)[sweep].at[ch, held(x)]

    edge_stiff = (es_ref, eside_ref)

    ends = zeros()
    for x in beyond:
        ends = to_edge(ends, stiff(x)[WINDOW, :], spot(x)[1])
    for tile, middle in ((0, cs_ref[...]), (1, ends)):
        others = beside_edge(edge_stiff[tile], edge_stiff[1 - tile][WINDOW, :], middle)
        for k, weight in enumerate(normalised(edge_stiff[tile][WINDOW, :], others)):
            ew_ref[k, tile] = weight
    for x in (-2, -1, 0, cells_x - 1, cells_x, cells_x + 1):
        own = stiff(x)[WINDOW, :]
        tile, g = spot(x)
        down, up = beside(own, from_edge(edge_stiff[tile][WINDOW, :], g))
        others = (
            stiff(x - 1)[WINDOW, :],
            stiff(x + 1)[WINDOW, :],
            stiff(x)[BEFORE, :],
            stiff(x)[AFTER, :],
            down,
            up,
        )
        for k, weight in enumerate(normalised(own, others)):
            hw_ref[k, held(x)] = weight

    for sweep in range(SWEEPS):
        last = sweep == SWEEPS - 1
        planes = [x for p in range(HALO) for x in (sweep - 2 + p, cells_x + 1 - sweep - p)]
        for x in planes:
            tile, g = spot(x)
            if 1 <= x < cells_x - 1:
                weights = [w_ref[k, x] for k in range(6)]
            else:
                weights = [hw_ref[k, held(x)] for k in range(6)]
            for ch in range(3):
                here = field(sweep, ch, x)
                own = here[WINDOW, :]
                down, up = beside(own, from_edge(e_ref[sweep, ch, tile, WINDOW, :], g))
                others = (
                    field(sweep, ch, x - 1)[WINDOW, :],
                    field(sweep, ch, x + 1)[WINDOW, :],
                    here[BEFORE, :],
                    here[AFTER, :],
                    down,
                    up,
                )
                new = jnp.where(first, own, relaxed(own, others, weights))
                if last:
                    place = x if x < HALO else x - cells_x + 2 * HALO
                    new_ref[ch, place] = new[2 : 2 + cells_y]
                    sem = sems.at[3 + 6 * ch + place]
                    copies.append(pltpu.make_async_copy(new_ref.at[ch, place], out_ref.at[ch, x], sem))
                    copies[-1].start()
                else:
                    (h1_ref, h2_ref)[sweep][ch, held(x), WINDOW, :] = new
        if last:
            break
        for ch in range(3):
            if sweep == 0:
                ends = zeros()
                for x in beyond:
                    ends = to_edge(ends, field(0, ch, x)[WINDOW, :], spot(x)[1])
                middles = (c_ref[0, ch], ends)
            else:
                ends = c_ref[1, ch]
                for x in (0, cells_x - 1):
                    ends = to_edge(ends, field(1, ch, x)[WINDOW, :], x)
                middles = (ends,)
            for tile, middle in enumerate(middles):
                others = beside_edge(e_ref.at[sweep, ch, tile], e_ref[sweep, ch, 1 - tile, WINDOW, :], middle)
                weights = [ew_ref[k, tile] for k in range(6)]
                e_ref[sweep + 1, ch, tile, WINDOW, :] = relaxed(
                    e_ref[sweep, ch, tile, WINDOW, :], others, weights
                )
    for copy in copies:
        copy.wait()


def step(value, axis, by):
    size = lax.axis_size(axis)
    return lax.ppermute(value, axis, [(i, i + by) for i in range(size) if 0 <= i + by < size])


def body(centre_coef, centre_index, stiff_factor, prev_disp):
    cells_x, cells_y, cells_z = stiff_factor.shape
    count_x = cells_x * lax.axis_size("gx")
    count_y = cells_y * lax.axis_size("gy")
    count_z = cells_z * lax.axis_size("gz")
    blocks = lax.axis_size("gx") * lax.axis_size("gy")
    depth = lax.axis_size("gz")
    scratch = pltpu.VMEM
    num = jnp.float32

    rows_y = 4 * cells_x * HALO
    rows, low, high, ylow, yhigh = kernel_call(
        functools.partial(begin_kernel, float(count_z)),
        "pack_z",
        (
            f32(blocks, LANES),
            f32(2, cells_y, LANES),
            f32(2, cells_y, LANES),
            f32(rows_y, LANES),
            f32(rows_y, LANES),
        ),
        2000 * MEGA,
        (),
        (
            scratch((3, cells_x, cells_y, LANES), num),
            scratch((cells_x, cells_y, LANES), num),
            scratch((4, cells_y, LANES), num),
            scratch((3, centre_index.shape[0]), num),
            scratch((1, centre_index.shape[0]), jnp.int32),
            pltpu.SemaphoreType.DMA((6,)),
        ),
        far=tuple(in_hbm(a) for a in (prev_disp, stiff_factor, centre_coef.T, centre_index[None])),
    )
    centres = lax.all_to_all(rows.reshape(blocks, 1, LANES), ("gx", "gy"), 0, 0, tiled=True)
    zabove, zbelow = step(low, "gz", -1), step(high, "gz", 1)

    rows_all = -(-(rows_y + 4 * HALO) // 8) * 8
    edge, ylow, yhigh = kernel_call(
        pack_y_kernel,
        "pack_y",
        (f32(4, cells_y, LANES), f32(rows_all, LANES), f32(rows_all, LANES)),
        300 * MEGA,
        (zabove, zbelow, ylow, yhigh),
    )
    yabove, ybelow = step(ylow, "gy", -1), step(yhigh, "gy", 1)

    table = stencil(count_x, count_y, count_z)
    (share,) = kernel_call(
        functools.partial(rbf_kernel, table, cells_x, cells_y, count_y),
        "rbf",
        (f32(depth, HALF, LANES),),
        1500 * MEGA,
        (centres.reshape(blocks, LANES),),
        (scratch((ROWS, LANES), num),),
        after=(ylow,),
    )
    shares = lax.all_to_all(share, "gz", 0, 0, tiled=True)

    xlow, xhigh = kernel_call(
        functools.partial(pack_x_kernel, float(count_z)),
        "pack_x",
        (f32(4 * HALO + 1, WIN, LANES), f32(4 * HALO + 1, WIN, LANES)),
        8000 * MEGA,
        (edge, yabove, ybelow, prev_disp, stiff_factor),
        (scratch((4, WIN, LANES), num),),
    )
    xabove, xbelow = step(xlow, "gx", -1), step(xhigh, "gx", 1)

    u0, u1, u2, s, w, es, cs, c, rbf, wide, done = kernel_call(
        functools.partial(inner_kernel, float(count_z)),
        "inner",
        (
            near(3, cells_x, ROWS, LANES),
            near(3, cells_x, ROWS, LANES),
            near(3, cells_x, ROWS, LANES),
            near(cells_x, ROWS, LANES),
            near(6, cells_x, WIN, LANES),
            near(ROWS, LANES),
            near(WIN, LANES),
            near(2, 3, WIN, LANES),
            near(WIN, LANES),
            near(4, WIN, LANES),
            near(3, cells_x, cells_y, cells_z),
        ),
        9000 * MEGA,
        (prev_disp, stiff_factor, in_hbm(edge), yabove, ybelow, shares),
        (
            scratch((3, 3, ROWS, LANES), num),
            scratch((6, WIN, LANES), num),
        ),
    )

    (out,) = kernel_call(
        outer_kernel,
        "outer",
        (Far((3, cells_x, cells_y, cells_z), num),),
        5500 * MEGA,
        (u0, u1, u2, s, w, wide, es, cs, c, rbf, done, xabove, xbelow),
        (
            scratch((3, 12, ROWS, LANES), num),
            scratch((3, 12, ROWS, LANES), num),
            scratch((3, 12, ROWS, LANES), num),
            scratch((12, ROWS, LANES), num),
            scratch((6, 12, WIN, LANES), num),
            scratch((3, 3, 2, ROWS, LANES), num),
            scratch((ROWS, LANES), num),
            scratch((6, 2, WIN, LANES), num),
            scratch((3, 2 * HALO, cells_y, LANES), num),
            pltpu.SemaphoreType.DMA((21,)),
        ),
    )
    return out


def solution(mesh):
    placed = (
        P(("gx", "gy", "gz"), None),
        P(("gx", "gy", "gz")),
        P("gx", "gy", "gz"),
        P(None, "gx", "gy", "gz"),
    )
    return jax.shard_map(
        body, mesh=mesh, in_specs=placed, out_specs=P(None, "gx", "gy", "gz"), check_vma=False
    )
```

```python
import functools
import math

import jax
import jax.numpy as jnp
from jax import lax
from jax.experimental import pallas as pl
from jax.experimental.pallas import tpu as pltpu
from jax.sharding import PartitionSpec as P

SWEEPS = 3
RADIUS = 0.02
OMEGA = 0.8

HALO = 3
TOP = 8
WIN = 72
HALF = 40
ROWS = 88
LANES = 128
MEGA = 1_100_000
VMEM_LIMIT = 16 * 1024 * 1024


def lane_ids(rows=WIN):
    return lax.broadcasted_iota(jnp.int32, (rows, LANES), 1)


def roll_lanes(value, shift):
    if not isinstance(shift, int):
        return pltpu.roll(value, shift % LANES, 1)
    return pltpu.roll(value, shift % LANES, 1) if shift % LANES else value


def kernel_call(kernel, name, outs, flops, args, scratch=(), after=(), far=(), aliases=None):
    moved = sum(math.prod(a.shape) * 4 for a in (*args, *outs))
    anywhere = pl.BlockSpec(memory_space=pl.ANY)
    return pl.pallas_call(
        kernel,
        name=name,
        out_shape=outs,
        in_specs=[pl.BlockSpec(memory_space=pltpu.VMEM)] * len(args) + [anywhere] * (len(far) + len(after)),
        out_specs=tuple(anywhere if isinstance(o, Far) else pl.BlockSpec(memory_space=pltpu.VMEM) for o in outs),
        scratch_shapes=list(scratch),
        input_output_aliases=aliases or {},
        compiler_params=pltpu.CompilerParams(vmem_limit_bytes=VMEM_LIMIT),
        cost_estimate=pl.CostEstimate(flops=flops, bytes_accessed=moved, transcendentals=0),
    )(*args, *far, *after)


class Far(jax.ShapeDtypeStruct):
    pass


def f32(*shape):
    return jax.ShapeDtypeStruct(shape, jnp.float32)


def in_hbm(value):
    return pltpu.with_memory_space_constraint(value, pltpu.HBM)


def far_out(*shape):
    return pltpu.HBM(shape, jnp.float32)


def near(*shape):
    return pltpu.VMEM(shape, jnp.float32)


def wall_scale(count_z, cells_z):
    deep = (lax.axis_index("gz") * cells_z + lane_ids(1)).astype(jnp.float32) + 0.5
    return count_z / deep


def begin_kernel(
    count_z,
    prev_ref,
    stiff_ref,
    coefs_ref,
    indices_ref,
    rows_ref,
    low_ref,
    high_ref,
    ylow_ref,
    yhigh_ref,
    prevv_ref,
    raw_ref,
    edge_ref,
    coef_ref,
    index_ref,
    sems,
):
    _, cells_x, cells_y, cells_z = prevv_ref.shape
    copies = [pltpu.make_async_copy(prev_ref.at[ch], prevv_ref.at[ch], sems.at[ch]) for ch in range(3)]
    copies.append(pltpu.make_async_copy(stiff_ref, raw_ref, sems.at[3]))
    short = [
        pltpu.make_async_copy(coefs_ref, coef_ref, sems.at[4]),
        pltpu.make_async_copy(indices_ref, index_ref, sems.at[5]),
    ]
    for copy in short + copies:
        copy.start()
    for copy in short:
        copy.wait()
    row = jnp.concatenate(
        [coef_ref[f : f + 1, :] for f in range(3)] + [index_ref[...].astype(jnp.float32)], axis=1
    )
    rows_ref[...] = jnp.broadcast_to(row, rows_ref.shape)
    scale = wall_scale(count_z, cells_z)
    lane = lax.broadcasted_iota(jnp.int32, (8, LANES), 1)
    place = lane % 8
    pick = jnp.where(place <= 3, jnp.clip(3 - place, 0, 2), cells_z - 1 - jnp.clip(place - 4, 0, 2))
    for ch in range(4):
        copies[ch].wait()
        for tile in range(cells_y // 8):
            rows = pl.ds(8 * tile, 8)
            edge = jnp.zeros((8, LANES), jnp.float32)
            for x in range(cells_x):
                if ch < 3:
                    value = prevv_ref[ch, x, rows, :]
                else:
                    value = raw_ref[x, rows, :] * scale
                picked = jnp.take_along_axis(value, pick, axis=1)
                edge = jnp.where(lane // 8 == x, picked, edge)
            edge_ref[ch, rows, :] = edge
        for x in range(cells_x):
            at = pl.ds((ch * cells_x + x) * HALO, HALO)
            plane = prevv_ref.at[ch, x] if ch < 3 else raw_ref.at[x]
            factor = 1.0 if ch < 3 else scale
            ylow_ref[at, :] = plane[:HALO, :] * factor
            yhigh_ref[at, :] = plane[cells_y - HALO :, :] * factor
    place = lane_ids(cells_y) % 8
    for pair in range(2):
        even, odd = edge_ref[2 * pair], edge_ref[2 * pair + 1]
        low_ref[pair] = jnp.where(place <= 3, even, roll_lanes(odd, 3))
        high_ref[pair] = jnp.where(place >= 4, even, roll_lanes(odd, -3))


def pack_y_kernel(above_ref, below_ref, ylow_ref, yhigh_ref, edge_ref, outlow_ref, outhigh_ref):
    rows = above_ref.shape[1]
    place = lane_ids(rows) % 8
    upper = (place >= 1) & (place <= 3)
    lower = (place >= 4) & (place <= 6)
    base = ylow_ref.shape[0]
    outlow_ref[:base, :] = ylow_ref[...]
    outhigh_ref[:base, :] = yhigh_ref[...]
    for ch in range(4):
        above, below = above_ref[ch // 2], below_ref[ch // 2]
        if ch % 2:
            above, below = roll_lanes(above, -3), roll_lanes(below, 3)
        edge = jnp.where(upper, above, jnp.where(lower, below, 0.0))
        edge_ref[ch] = edge
        at = pl.ds(base + ch * HALO, HALO)
        outlow_ref[at, :] = edge[:HALO]
        outhigh_ref[at, :] = edge[rows - HALO :]
    rest = outlow_ref.shape[0] - base - 4 * HALO
    outlow_ref[base + 4 * HALO :, :] = jnp.zeros((rest, LANES), jnp.float32)
    outhigh_ref[base + 4 * HALO :, :] = jnp.zeros((rest, LANES), jnp.float32)


def fill(out, below_ref, middle, above_ref, at):
    cells_y = middle.shape[0]
    out[0:2, :] = below_ref[at + 1 : at + HALO, :]
    out[2 : 2 + cells_y, :] = middle
    out[2 + cells_y : 2 + cells_y + HALO, :] = above_ref[at : at + HALO, :]
    out[2 + cells_y + HALO : WIN, :] = jnp.zeros((WIN - 2 - cells_y - HALO, LANES), jnp.float32)


def pack_x_kernel(
    count_z, edge_ref, yabove_ref, ybelow_ref, prev_ref, stiff_ref, low_ref, high_ref, wide_ref
):
    _, cells_x, cells_y, cells_z = prev_ref.shape
    scale = wall_scale(count_z, cells_z)
    lane = lane_ids()
    base = 4 * cells_x * HALO
    low = jnp.zeros((WIN, LANES), jnp.float32)
    high = low

    for ch in range(4):
        fill(wide_ref.at[ch], ybelow_ref, edge_ref[ch], yabove_ref, base + ch * HALO)
        turned = roll_lanes(wide_ref[ch], 32 * ch)
        at_low = (lane - 32 * ch) & (LANES - 1)
        low = jnp.where(at_low < 8 * HALO, turned, low)
        high = jnp.where(at_low >= LANES - 8 * HALO, turned, high)
    low_ref[4 * HALO] = low
    high_ref[4 * HALO] = high
    for side, out in enumerate((low_ref, high_ref)):
        for ch in range(4):
            for p in range(HALO):
                x = p + side * (cells_x - HALO)
                middle = prev_ref[ch, x] if ch < 3 else stiff_ref[x] * scale
                fill(out.at[ch * HALO + p], ybelow_ref, middle, yabove_ref, (ch * cells_x + x) * HALO)


def stencil(count_x, count_y, count_z):
    table = {}
    for step_x in range(int(RADIUS * count_x) + 2):
        for step_y in range(int(RADIUS * count_y) + 2):
            square = (step_x / count_x) ** 2 + (step_y / count_y) ** 2 + (0.5 / count_z) ** 2
            ratio = math.sqrt(square) / RADIUS
            lead = max(1.0 - ratio, 0.0)
            if lead > 0.0:
                table[step_x, step_y] = lead**4 * (4.0 * ratio + 1.0)
    return table


REACH_X = 8
REACH_Y = 8
GRID_X = 32
GRID_Y = 80


def rbf_kernel(table, cells_x, cells_y, count_y, centres_ref, _, out_ref, grid_ref):
    slots = centres_ref.shape[0] // 4
    first_x = (lax.axis_index("gx") * cells_x - REACH_X).astype(jnp.float32)
    first_y = (lax.axis_index("gy") * cells_y - REACH_Y).astype(jnp.float32)
    quarter = lane_ids(slots) // 32
    fields = []
    for f in range(4):
        field = jnp.zeros((slots, LANES), jnp.float32)
        for k in range(4):
            part = roll_lanes(centres_ref[k * slots : (k + 1) * slots, :], 32 * (k - f))
            field = jnp.where(quarter == k, part, field)
        fields.append(field)
    index = fields[3]
    at_x = jnp.floor(index * (1.0 / count_y))
    at_y = index - at_x * count_y - first_y
    at_x = at_x - first_x
    heads = [f.astype(jnp.bfloat16).astype(jnp.float32) for f in fields[:3]]
    tails = [f - h for f, h in zip(fields[:3], heads)]
    row_y = lax.broadcasted_iota(jnp.int32, (GRID_Y, LANES), 0).astype(jnp.float32)
    row_x = lax.broadcasted_iota(jnp.int32, (GRID_X, LANES), 0).astype(jnp.float32)
    total = jnp.zeros((GRID_Y, 2 * LANES), jnp.float32)
    blank = jnp.zeros((LANES - 3 * GRID_X, LANES), jnp.float32)
    for q in range(0, slots, 2):
        left, right = [], []
        for r in (q, q + 1):
            hit_y = at_y[r : r + 1, :] == row_y
            hit_x = at_x[r : r + 1, :] == row_x
            left.append(jnp.where(hit_y, 1.0, 0.0).astype(jnp.bfloat16))
            pieces = []
            for group in (heads, tails):
                pieces += [jnp.where(hit_x, g[r : r + 1, :], 0.0) for g in group]
                pieces.append(blank)
            right.append(jnp.concatenate(pieces, axis=0).astype(jnp.bfloat16))
        total = total + lax.dot_general(
            jnp.concatenate(left, axis=1),
            jnp.concatenate(right, axis=1),
            (((1,), (1,)), ((), ())),
            preferred_element_type=jnp.float32,
        )
    grid = total[:, :LANES] + total[:, LANES:]
    reach_x = max(a for a, _ in table)
    reach_y = max(b for _, b in table)
    result = jnp.zeros((WIN, LANES), jnp.float32)
    for step_x in range(reach_x + 1):
        value = roll_lanes(grid, 2 - REACH_X + step_x)
        if step_x:
            value = value + roll_lanes(grid, 2 - REACH_X - step_x)
        grid_ref[:GRID_Y, :] = value
        for step_y in range(reach_y + 1):
            phi = table.get((step_x, step_y))
            if phi is None:
                continue
            start = REACH_Y - 2
            part = grid_ref[start + step_y : start + step_y + WIN, :]
            if step_y:
                part = part + grid_ref[start - step_y : start - step_y + WIN, :]
            result = result + phi * part
    lane = lane_ids()
    width = cells_x + 4
    close = jnp.where(
        lane < width,
        result,
        jnp.where(lane < 2 * width, roll_lanes(result, width - 32), roll_lanes(result, 2 * (width - 32))),
    )
    half = out_ref.shape[1]
    share = jnp.where(lane_ids(half) < LANES // 2, close[:half], roll_lanes(close[WIN - half :], LANES // 2))
    for k in range(out_ref.shape[0]):
        out_ref[k] = share


WINDOW = pl.ds(TOP, WIN)
BEFORE = pl.ds(TOP - 1, WIN)
AFTER = pl.ds(TOP + 1, WIN)


def spot(x):
    if isinstance(x, int):
        return (0 if 0 <= x < 16 else 1), x % 16
    return 0, x


def beside(value, edge):
    lane = lane_ids(value.shape[0])
    down = jnp.where(lane == 0, edge, roll_lanes(value, 1))
    up = jnp.where(lane == LANES - 1, edge, roll_lanes(value, -1))
    return down, up


def from_edge(tile, g):
    return roll_lanes(tile, LANES - 4 - 8 * g)


def to_edge(old, plane, g):
    lane = lane_ids()
    here = (lane // 8 == g) & ((lane % 8 == 3) | (lane % 8 == 4))
    return jnp.where(here, roll_lanes(plane, 8 * g + 4), old)


def beside_edge(own_ref, other, middle):
    lane = lane_ids()
    place = lane % 8
    own = own_ref[WINDOW, :]
    left = jnp.where(lane >= 8, roll_lanes(own, 8), roll_lanes(other, 8))
    right = jnp.where(lane < LANES - 8, roll_lanes(own, -8), roll_lanes(other, -8))
    minus = jnp.where(place == 4, middle, roll_lanes(own, 1))
    plus = jnp.where(place == 3, middle, roll_lanes(own, -1))
    return left, right, own_ref[BEFORE, :], own_ref[AFTER, :], minus, plus


def normalised(own, others):
    faces = [0.5 * (own + other) for other in others]
    total = functools.reduce(lambda a, b: a + b, faces)
    inside = own > 0.0
    factor = jnp.where(inside, OMEGA / jnp.where(inside, total, 1.0), 0.0)
    return [face * factor for face in faces]


def relaxed(own, others, weights):
    new = (1.0 - OMEGA) * own
    for weight, other in zip(weights, others):
        new = new + weight * other
    return new


def zeros():
    return jnp.zeros((WIN, LANES), jnp.float32)


def wall_lane():
    return (lane_ids() == 0) & (lax.axis_index("gz") == 0)


def column_of(rbf, ch, x, cells_x):
    return roll_lanes(rbf, 2 * LANES - 2 - (cells_x + 4) * ch - x)


def inner_kernel(
    count_z, prev_ref, stiff_ref, edge_ref, yabove_ref, ybelow_ref, shares_ref,
    u0_ref, u1_ref, u2_ref, s_ref, w_ref, es_ref, cs_ref, c_ref, rbf_ref, widev_ref, done_ref,
    e_ref, ew_ref,
):
    _, cells_x, cells_y, cells_z = prev_ref.shape
    first = wall_lane()
    scale = wall_scale(count_z, cells_z)
    main = pl.ds(TOP + 2, cells_y)

    def assemble(ch, x):
        at = (ch * cells_x + x) * HALO
        plane = u0_ref.at[ch, x] if ch < 3 else s_ref.at[x]
        plane[main, :] = prev_ref[ch, x] if ch < 3 else stiff_ref[x] * scale
        plane[TOP - 1 : TOP + 2, :] = ybelow_ref[at : at + HALO, :]
        plane[TOP + 2 + cells_y : TOP + 2 + cells_y + HALO, :] = yabove_ref[at : at + HALO, :]

    for x in range(cells_x):
        assemble(3, x)
    for ch in range(4):
        fill(widev_ref.at[ch], ybelow_ref, edge_ref[ch], yabove_ref, (4 * cells_x + ch) * HALO)
    es_ref[WINDOW, :] = widev_ref[3]
    ends = zeros()
    for x in range(cells_x):
        ends = to_edge(ends, s_ref[x, WINDOW, :], x)
    cs_ref[...] = ends

    def weigh(x, carry):
        own = s_ref[x, WINDOW, :]
        down, up = beside(own, from_edge(es_ref[WINDOW, :], x))
        others = (s_ref[x - 1, WINDOW, :], s_ref[x + 1, WINDOW, :], s_ref[x, BEFORE, :], s_ref[x, AFTER, :], down, up)
        for k, weight in enumerate(normalised(own, others)):
            w_ref[k, x] = weight
        return carry

    for x in range(1, cells_x - 1):
        weigh(x, 0)
    others = beside_edge(es_ref, zeros(), cs_ref[...])
    for k, weight in enumerate(normalised(es_ref[WINDOW, :], others)):
        ew_ref[k] = weight

    for ch in range(3):
        e_ref[0, ch, WINDOW, :] = widev_ref[ch]
        for x in range(cells_x):
            assemble(ch, x)
    rbf_ref[...] = zeros()

    @pl.when(lax.axis_index("gz") == 0)
    def _():
        share = shares_ref[0]
        for k in range(1, shares_ref.shape[0]):
            share = share + shares_ref[k]
        half = share.shape[0]
        rbf_ref[WIN - half :, :] = roll_lanes(share, LANES // 2)
        rbf_ref[:half, :] = share
        rbf = rbf_ref[...]

        def layer(x, carry):
            own = first & (s_ref[x, WINDOW, :] > 0.0)
            for ch in range(3):
                column = column_of(rbf, ch, x, cells_x)
                u0_ref[ch, x, WINDOW, :] = jnp.where(own, column, u0_ref[ch, x, WINDOW, :])
            return carry

        for x in range(cells_x):
            layer(x, 0)

    stages = (u0_ref, u1_ref, u2_ref)
    for sweep in range(SWEEPS):
        now, last = stages[sweep], sweep == SWEEPS - 1

        rows, weigh_rows, above, below, held = (
            (pl.ds(TOP + 2, cells_y), pl.ds(2, cells_y), pl.ds(TOP + 1, cells_y), pl.ds(TOP + 3, cells_y), first[:cells_y])
            if last
            else (WINDOW, pl.ds(0, WIN), BEFORE, AFTER, first)
        )
        for x in range(1 + sweep, cells_x - 1 - sweep):
            weights = [w_ref[k, x, weigh_rows, :] for k in range(6)]
            for ch in range(3):
                own = now[ch, x, rows, :]
                down, up = beside(own, from_edge(e_ref[sweep, ch, rows, :], x))
                others = (
                    now[ch, x - 1, rows, :],
                    now[ch, x + 1, rows, :],
                    now[ch, x, above, :],
                    now[ch, x, below, :],
                    down,
                    up,
                )
                new = jnp.where(held, own, relaxed(own, others, weights))
                if last:
                    done_ref[ch, x] = new
                else:
                    stages[sweep + 1][ch, x, WINDOW, :] = new
        if not last:
            for ch in range(3):
                ends = zeros()
                for x in range(sweep, cells_x - sweep):
                    ends = to_edge(ends, now[ch, x, WINDOW, :], x)
                c_ref[sweep, ch] = ends
                others = beside_edge(e_ref.at[sweep, ch], zeros(), ends)
                weights = [ew_ref[k] for k in range(6)]
                e_ref[sweep + 1, ch, WINDOW, :] = relaxed(e_ref[sweep, ch, WINDOW, :], others, weights)


def outer_kernel(
    u0_ref, u1_ref, u2_ref, s_ref, w_ref, wide_ref, es_ref, cs_ref, c_ref, rbf_ref, done_ref, xabove_ref, xbelow_ref,
    out_ref,
    h0_ref, h1_ref, h2_ref, hs_ref, hw_ref, e_ref, eside_ref, ew_ref, new_ref, sems,
):
    _, cells_x, _, _ = u0_ref.shape
    cells_y = done_ref.shape[2]
    lane = lane_ids()
    first = wall_lane()
    inside = pl.ds(HALO, cells_x - 2 * HALO)
    copies = [pltpu.make_async_copy(done_ref.at[ch, inside], out_ref.at[ch, inside], sems.at[ch]) for ch in range(3)]
    for copy in copies:
        copy.start()

    def held(x):
        return x + HALO if x < HALO else x - cells_x + HALO + 6

    beyond = [x for p in range(HALO) for x in (p - HALO, cells_x + p)]
    for x in beyond:
        source, p = (xbelow_ref, x + HALO) if x < 0 else (xabove_ref, x - cells_x)
        own = source[3 * HALO + p]
        hs_ref[held(x), WINDOW, :] = own
        for ch in range(3):
            column = column_of(rbf_ref[...], ch, x, cells_x)
            h0_ref[ch, held(x), WINDOW, :] = jnp.where(first & (own > 0.0), column, source[ch * HALO + p])
    for ch in range(4):
        above = roll_lanes(xabove_ref[4 * HALO], -32 * ch)
        below = roll_lanes(xbelow_ref[4 * HALO], -32 * ch)
        side = jnp.where(lane < 8 * HALO, above, jnp.where(lane >= LANES - 8 * HALO, below, 0.0))
        if ch < 3:
            e_ref[0, ch, 0, WINDOW, :] = wide_ref[ch]
            e_ref[0, ch, 1, WINDOW, :] = side
        else:
            eside_ref[WINDOW, :] = side

    def stiff(x):
        return s_ref.at[x] if 0 <= x < cells_x else hs_ref.at[held(x)]

    def field(sweep, ch, x):
        if sweep <= x < cells_x - sweep:
            return (u0_ref, u1_ref, u2_ref)[sweep].at[ch, x]
        return (h0_ref, h1_ref, h2_ref)[sweep].at[ch, held(x)]

    edge_stiff = (es_ref, eside_ref)

    ends = zeros()
    for x in (-1, cells_x):
        ends = to_edge(ends, stiff(x)[WINDOW, :], spot(x)[1])
    for tile, middle in ((0, cs_ref[...]), (1, ends)):
        others = beside_edge(edge_stiff[tile], edge_stiff[1 - tile][WINDOW, :], middle)
        for k, weight in enumerate(normalised(edge_stiff[tile][WINDOW, :], others)):
            ew_ref[k, tile] = weight
    for x in (-2, -1, 0, cells_x - 1, cells_x, cells_x + 1):
        own = stiff(x)[WINDOW, :]
        tile, g = spot(x)
        down, up = beside(own, from_edge(edge_stiff[tile][WINDOW, :], g))
        others = (
            stiff(x - 1)[WINDOW, :],
            stiff(x + 1)[WINDOW, :],
            stiff(x)[BEFORE, :],
            stiff(x)[AFTER, :],
            down,
            up,
        )
        for k, weight in enumerate(normalised(own, others)):
            hw_ref[k, held(x)] = weight

    for sweep in range(SWEEPS):
        last = sweep == SWEEPS - 1
        rows, weigh_rows, above, below, fixed = (
            (pl.ds(TOP + 2, cells_y), pl.ds(2, cells_y), pl.ds(TOP + 1, cells_y), pl.ds(TOP + 3, cells_y), first[:cells_y])
            if last
            else (WINDOW, pl.ds(0, WIN), BEFORE, AFTER, first)
        )
        planes = [x for p in range(HALO) for x in (sweep - 2 + p, cells_x + 1 - sweep - p)]
        for x in planes:
            tile, g = spot(x)
            if 1 <= x < cells_x - 1:
                weights = [w_ref[k, x, weigh_rows, :] for k in range(6)]
            else:
                weights = [hw_ref[k, held(x), weigh_rows, :] for k in range(6)]
            for ch in range(3):
                here = field(sweep, ch, x)
                own = here[rows, :]
                down, up = beside(own, from_edge(e_ref[sweep, ch, tile, rows, :], g))
                others = (
                    field(sweep, ch, x - 1)[rows, :],
                    field(sweep, ch, x + 1)[rows, :],
                    here[above, :],
                    here[below, :],
                    down,
                    up,
                )
                new = jnp.where(fixed, own, relaxed(own, others, weights))
                if last:
                    place = x if x < HALO else x - cells_x + 2 * HALO
                    new_ref[ch, place] = new
                    sem = sems.at[3 + 6 * ch + place]
                    copies.append(pltpu.make_async_copy(new_ref.at[ch, place], out_ref.at[ch, x], sem))
                    copies[-1].start()
                else:
                    (h1_ref, h2_ref)[sweep][ch, held(x), WINDOW, :] = new
        if last:
            break
        for ch in range(3):
            if sweep == 0:
                ends = zeros()
                for x in (-1, cells_x):
                    ends = to_edge(ends, field(0, ch, x)[WINDOW, :], spot(x)[1])
                middles = (c_ref[0, ch], ends)
            else:
                ends = c_ref[1, ch]
                for x in (0, cells_x - 1):
                    ends = to_edge(ends, field(1, ch, x)[WINDOW, :], x)
                middles = (ends,)
            for tile, middle in enumerate(middles):
                others = beside_edge(e_ref.at[sweep, ch, tile], e_ref[sweep, ch, 1 - tile, WINDOW, :], middle)
                weights = [ew_ref[k, tile] for k in range(6)]
                e_ref[sweep + 1, ch, tile, WINDOW, :] = relaxed(
                    e_ref[sweep, ch, tile, WINDOW, :], others, weights
                )
    for copy in copies:
        copy.wait()


def step(value, axis, by):
    size = lax.axis_size(axis)
    return lax.ppermute(value, axis, [(i, i + by) for i in range(size) if 0 <= i + by < size])


def body(centre_coef, centre_index, stiff_factor, prev_disp):
    cells_x, cells_y, cells_z = stiff_factor.shape
    count_x = cells_x * lax.axis_size("gx")
    count_y = cells_y * lax.axis_size("gy")
    count_z = cells_z * lax.axis_size("gz")
    blocks = lax.axis_size("gx") * lax.axis_size("gy")
    depth = lax.axis_size("gz")
    scratch = pltpu.VMEM
    num = jnp.float32

    rows_y = 4 * cells_x * HALO
    rows, low, high, ylow, yhigh = kernel_call(
        functools.partial(begin_kernel, float(count_z)),
        "pack_z",
        (
            f32(blocks, LANES),
            f32(2, cells_y, LANES),
            f32(2, cells_y, LANES),
            f32(rows_y, LANES),
            f32(rows_y, LANES),
        ),
        2000 * MEGA,
        (),
        (
            scratch((3, cells_x, cells_y, LANES), num),
            scratch((cells_x, cells_y, LANES), num),
            scratch((4, cells_y, LANES), num),
            scratch((3, centre_index.shape[0]), num),
            scratch((1, centre_index.shape[0]), jnp.int32),
            pltpu.SemaphoreType.DMA((6,)),
        ),
        far=tuple(in_hbm(a) for a in (prev_disp, stiff_factor, centre_coef.T, centre_index[None])),
    )
    centres = lax.all_to_all(rows.reshape(blocks, 1, LANES), ("gx", "gy"), 0, 0, tiled=True)
    zabove, zbelow = step(low, "gz", -1), step(high, "gz", 1)

    rows_all = -(-(rows_y + 4 * HALO) // 8) * 8
    edge, ylow, yhigh = kernel_call(
        pack_y_kernel,
        "pack_y",
        (f32(4, cells_y, LANES), f32(rows_all, LANES), f32(rows_all, LANES)),
        300 * MEGA,
        (zabove, zbelow, ylow, yhigh),
    )
    yabove, ybelow = step(ylow, "gy", -1), step(yhigh, "gy", 1)

    table = stencil(count_x, count_y, count_z)
    (share,) = kernel_call(
        functools.partial(rbf_kernel, table, cells_x, cells_y, count_y),
        "rbf",
        (f32(depth, HALF, LANES),),
        1500 * MEGA,
        (centres.reshape(blocks, LANES),),
        (scratch((ROWS, LANES), num),),
        after=(ylow,),
    )
    shares = lax.all_to_all(share, "gz", 0, 0, tiled=True)

    xlow, xhigh = kernel_call(
        functools.partial(pack_x_kernel, float(count_z)),
        "pack_x",
        (far_out(4 * HALO + 1, WIN, LANES), far_out(4 * HALO + 1, WIN, LANES)),
        8000 * MEGA,
        (edge, yabove, ybelow, prev_disp, stiff_factor),
        (scratch((4, WIN, LANES), num),),
    )
    xabove, xbelow = step(xlow, "gx", -1), step(xhigh, "gx", 1)

    u0, u1, u2, s, w, es, cs, c, rbf, wide, done = kernel_call(
        functools.partial(inner_kernel, float(count_z)),
        "inner",
        (
            near(3, cells_x, ROWS, LANES),
            near(3, cells_x, ROWS, LANES),
            near(3, cells_x, ROWS, LANES),
            near(cells_x, ROWS, LANES),
            near(6, cells_x, WIN, LANES),
            near(ROWS, LANES),
            near(WIN, LANES),
            near(2, 3, WIN, LANES),
            near(WIN, LANES),
            near(4, WIN, LANES),
            near(3, cells_x, cells_y, cells_z),
        ),
        9000 * MEGA,
        (prev_disp, stiff_factor, in_hbm(edge), yabove, ybelow, shares),
        (
            scratch((3, 3, ROWS, LANES), num),
            scratch((6, WIN, LANES), num),
        ),
    )

    (out,) = kernel_call(
        outer_kernel,
        "outer",
        (Far((3, cells_x, cells_y, cells_z), num),),
        5500 * MEGA,
        (u0, u1, u2, s, w, wide, es, cs, c, rbf, done, xabove, xbelow),
        (
            scratch((3, 12, ROWS, LANES), num),
            scratch((3, 12, ROWS, LANES), num),
            scratch((3, 12, ROWS, LANES), num),
            scratch((12, ROWS, LANES), num),
            scratch((6, 12, WIN, LANES), num),
            scratch((3, 3, 2, ROWS, LANES), num),
            scratch((ROWS, LANES), num),
            scratch((6, 2, WIN, LANES), num),
            scratch((3, 2 * HALO, cells_y, LANES), num),
            pltpu.SemaphoreType.DMA((21,)),
        ),
    )
    return out


def solution(mesh):
    placed = (
        P(("gx", "gy", "gz"), None),
        P(("gx", "gy", "gz")),
        P("gx", "gy", "gz"),
        P(None, "gx", "gy", "gz"),
    )
    return jax.shard_map(
        body, mesh=mesh, in_specs=placed, out_specs=P(None, "gx", "gy", "gz"), check_vma=False
    )
```

```python
import functools
import math

import jax
import jax.numpy as jnp
from jax import lax
from jax.experimental import pallas as pl
from jax.experimental.pallas import tpu as pltpu
from jax.sharding import PartitionSpec as P

SWEEPS = 3
RADIUS = 0.02
OMEGA = 0.8

HALO = 3
TOP = 8
WIN = 72
HALF = 40
ROWS = 88
LANES = 128
MEGA = 1_100_000
VMEM_LIMIT = 16 * 1024 * 1024


def lane_ids(rows=WIN):
    return lax.broadcasted_iota(jnp.int32, (rows, LANES), 1)


def roll_lanes(value, shift):
    if not isinstance(shift, int):
        return pltpu.roll(value, shift % LANES, 1)
    return pltpu.roll(value, shift % LANES, 1) if shift % LANES else value


def kernel_call(kernel, name, outs, flops, args, scratch=(), after=(), far=(), aliases=None):
    moved = sum(math.prod(a.shape) * 4 for a in (*args, *outs))
    anywhere = pl.BlockSpec(memory_space=pl.ANY)
    return pl.pallas_call(
        kernel,
        name=name,
        out_shape=outs,
        in_specs=[pl.BlockSpec(memory_space=pltpu.VMEM)] * len(args) + [anywhere] * (len(far) + len(after)),
        out_specs=tuple(anywhere if isinstance(o, Far) else pl.BlockSpec(memory_space=pltpu.VMEM) for o in outs),
        scratch_shapes=list(scratch),
        input_output_aliases=aliases or {},
        compiler_params=pltpu.CompilerParams(vmem_limit_bytes=VMEM_LIMIT),
        cost_estimate=pl.CostEstimate(flops=flops, bytes_accessed=moved, transcendentals=0),
    )(*args, *far, *after)


class Far(jax.ShapeDtypeStruct):
    pass


def f32(*shape):
    return jax.ShapeDtypeStruct(shape, jnp.float32)


def in_hbm(value):
    return pltpu.with_memory_space_constraint(value, pltpu.HBM)


def far_out(*shape):
    return pltpu.HBM(shape, jnp.float32)


def near(*shape):
    return pltpu.VMEM(shape, jnp.float32)


def wall_scale(count_z, cells_z):
    deep = (lax.axis_index("gz") * cells_z + lane_ids(1)).astype(jnp.float32) + 0.5
    return count_z / deep


def begin_kernel(
    count_z,
    prev_ref,
    stiff_ref,
    coefs_ref,
    indices_ref,
    rows_ref,
    low_ref,
    high_ref,
    ylow_ref,
    yhigh_ref,
    prevv_ref,
    raw_ref,
    edge_ref,
    coef_ref,
    index_ref,
    sems,
):
    _, cells_x, cells_y, cells_z = prevv_ref.shape
    copies = [pltpu.make_async_copy(prev_ref.at[ch], prevv_ref.at[ch], sems.at[ch]) for ch in range(3)]
    copies.append(pltpu.make_async_copy(stiff_ref, raw_ref, sems.at[3]))
    short = [
        pltpu.make_async_copy(coefs_ref, coef_ref, sems.at[4]),
        pltpu.make_async_copy(indices_ref, index_ref, sems.at[5]),
    ]
    for copy in short + copies:
        copy.start()
    for copy in short:
        copy.wait()
    row = jnp.concatenate(
        [coef_ref[f : f + 1, :] for f in range(3)] + [index_ref[...].astype(jnp.float32)], axis=1
    )
    rows_ref[...] = jnp.broadcast_to(row, rows_ref.shape)
    scale = wall_scale(count_z, cells_z)
    lane = lax.broadcasted_iota(jnp.int32, (8, LANES), 1)
    place = lane % 8
    pick = jnp.where(place <= 3, jnp.clip(3 - place, 0, 2), cells_z - 1 - jnp.clip(place - 4, 0, 2))
    for ch in range(4):
        copies[ch].wait()
        for tile in range(cells_y // 8):
            rows = pl.ds(8 * tile, 8)
            edge = jnp.zeros((8, LANES), jnp.float32)
            for x in range(cells_x):
                if ch < 3:
                    value = prevv_ref[ch, x, rows, :]
                else:
                    value = raw_ref[x, rows, :] * scale
                picked = jnp.take_along_axis(value, pick, axis=1)
                edge = jnp.where(lane // 8 == x, picked, edge)
            edge_ref[ch, rows, :] = edge
        for x in range(cells_x):
            at = pl.ds((ch * cells_x + x) * HALO, HALO)
            plane = prevv_ref.at[ch, x] if ch < 3 else raw_ref.at[x]
            factor = 1.0 if ch < 3 else scale
            ylow_ref[at, :] = plane[:HALO, :] * factor
            yhigh_ref[at, :] = plane[cells_y - HALO :, :] * factor
    place = lane_ids(cells_y) % 8
    for pair in range(2):
        even, odd = edge_ref[2 * pair], edge_ref[2 * pair + 1]
        low_ref[pair] = jnp.where(place <= 3, even, roll_lanes(odd, 3))
        high_ref[pair] = jnp.where(place >= 4, even, roll_lanes(odd, -3))


def pair_kernel(own_ref, other_ref, out_ref):
    rows = lax.broadcasted_iota(jnp.int32, out_ref.shape, 0)
    own, other = (jnp.broadcast_to(ref[0:1, :], out_ref.shape) for ref in (own_ref, other_ref))
    out_ref[...] = jnp.where(rows % 2 == 0, own, other)


def pack_y_kernel(above_ref, below_ref, ylow_ref, yhigh_ref, edge_ref, outlow_ref, outhigh_ref):
    rows = above_ref.shape[1]
    place = lane_ids(rows) % 8
    upper = (place >= 1) & (place <= 3)
    lower = (place >= 4) & (place <= 6)
    base = ylow_ref.shape[0]
    outlow_ref[:base, :] = ylow_ref[...]
    outhigh_ref[:base, :] = yhigh_ref[...]
    for ch in range(4):
        above, below = above_ref[ch // 2], below_ref[ch // 2]
        if ch % 2:
            above, below = roll_lanes(above, -3), roll_lanes(below, 3)
        edge = jnp.where(upper, above, jnp.where(lower, below, 0.0))
        edge_ref[ch] = edge
        at = pl.ds(base + ch * HALO, HALO)
        outlow_ref[at, :] = edge[:HALO]
        outhigh_ref[at, :] = edge[rows - HALO :]
    rest = outlow_ref.shape[0] - base - 4 * HALO
    outlow_ref[base + 4 * HALO :, :] = jnp.zeros((rest, LANES), jnp.float32)
    outhigh_ref[base + 4 * HALO :, :] = jnp.zeros((rest, LANES), jnp.float32)


def fill(out, below_ref, middle, above_ref, at):
    cells_y = middle.shape[0]
    out[0:2, :] = below_ref[at + 1 : at + HALO, :]
    out[2 : 2 + cells_y, :] = middle
    out[2 + cells_y : 2 + cells_y + HALO, :] = above_ref[at : at + HALO, :]
    out[2 + cells_y + HALO : WIN, :] = jnp.zeros((WIN - 2 - cells_y - HALO, LANES), jnp.float32)


def pack_x_kernel(
    count_z, edge_ref, yabove_ref, ybelow_ref, prev_ref, stiff_ref, low_ref, high_ref, wide_ref
):
    _, cells_x, cells_y, cells_z = prev_ref.shape
    scale = wall_scale(count_z, cells_z)
    lane = lane_ids()
    base = 4 * cells_x * HALO
    low = jnp.zeros((WIN, LANES), jnp.float32)
    high = low

    for ch in range(4):
        fill(wide_ref.at[ch], ybelow_ref, edge_ref[ch], yabove_ref, base + ch * HALO)
        turned = roll_lanes(wide_ref[ch], 32 * ch)
        at_low = (lane - 32 * ch) & (LANES - 1)
        low = jnp.where(at_low < 8 * HALO, turned, low)
        high = jnp.where(at_low >= LANES - 8 * HALO, turned, high)
    low_ref[4 * HALO] = low
    high_ref[4 * HALO] = high
    for side, out in enumerate((low_ref, high_ref)):
        for ch in range(4):
            for p in range(HALO):
                x = p + side * (cells_x - HALO)
                middle = prev_ref[ch, x] if ch < 3 else stiff_ref[x] * scale
                fill(out.at[ch * HALO + p], ybelow_ref, middle, yabove_ref, (ch * cells_x + x) * HALO)


def stencil(count_x, count_y, count_z):
    table = {}
    for step_x in range(int(RADIUS * count_x) + 2):
        for step_y in range(int(RADIUS * count_y) + 2):
            square = (step_x / count_x) ** 2 + (step_y / count_y) ** 2 + (0.5 / count_z) ** 2
            ratio = math.sqrt(square) / RADIUS
            lead = max(1.0 - ratio, 0.0)
            if lead > 0.0:
                table[step_x, step_y] = lead**4 * (4.0 * ratio + 1.0)
    return table


REACH_X = 8
REACH_Y = 8
GRID_X = 32
GRID_Y = 80


def rbf_kernel(table, cells_x, cells_y, count_y, centres_ref, _, out_ref, grid_ref):
    slots = centres_ref.shape[0] // 4
    first_x = (lax.axis_index("gx") * cells_x - REACH_X).astype(jnp.float32)
    first_y = (lax.axis_index("gy") * cells_y - REACH_Y).astype(jnp.float32)
    quarter = lane_ids(slots) // 32
    fields = []
    for f in range(4):
        field = jnp.zeros((slots, LANES), jnp.float32)
        for k in range(4):
            part = roll_lanes(centres_ref[k * slots : (k + 1) * slots, :], 32 * (k - f))
            field = jnp.where(quarter == k, part, field)
        fields.append(field)
    index = fields[3]
    at_x = jnp.floor(index * (1.0 / count_y))
    at_y = index - at_x * count_y - first_y
    at_x = at_x - first_x
    heads = [f.astype(jnp.bfloat16).astype(jnp.float32) for f in fields[:3]]
    tails = [f - h for f, h in zip(fields[:3], heads)]
    row_y = lax.broadcasted_iota(jnp.int32, (GRID_Y, LANES), 0).astype(jnp.float32)
    row_x = lax.broadcasted_iota(jnp.int32, (GRID_X, LANES), 0).astype(jnp.float32)
    total = jnp.zeros((GRID_Y, 2 * LANES), jnp.float32)
    blank = jnp.zeros((LANES - 3 * GRID_X, LANES), jnp.float32)
    for q in range(0, slots, 2):
        left, right = [], []
        for r in (q, q + 1):
            hit_y = at_y[r : r + 1, :] == row_y
            hit_x = at_x[r : r + 1, :] == row_x
            left.append(jnp.where(hit_y, 1.0, 0.0).astype(jnp.bfloat16))
            pieces = []
            for group in (heads, tails):
                pieces += [jnp.where(hit_x, g[r : r + 1, :], 0.0) for g in group]
                pieces.append(blank)
            right.append(jnp.concatenate(pieces, axis=0).astype(jnp.bfloat16))
        total = total + lax.dot_general(
            jnp.concatenate(left, axis=1),
            jnp.concatenate(right, axis=1),
            (((1,), (1,)), ((), ())),
            preferred_element_type=jnp.float32,
        )
    grid = total[:, :LANES] + total[:, LANES:]
    reach_x = max(a for a, _ in table)
    reach_y = max(b for _, b in table)
    result = jnp.zeros((WIN, LANES), jnp.float32)
    for step_x in range(reach_x + 1):
        value = roll_lanes(grid, 2 - REACH_X + step_x)
        if step_x:
            value = value + roll_lanes(grid, 2 - REACH_X - step_x)
        grid_ref[:GRID_Y, :] = value
        for step_y in range(reach_y + 1):
            phi = table.get((step_x, step_y))
            if phi is None:
                continue
            start = REACH_Y - 2
            part = grid_ref[start + step_y : start + step_y + WIN, :]
            if step_y:
                part = part + grid_ref[start - step_y : start - step_y + WIN, :]
            result = result + phi * part
    lane = lane_ids()
    width = cells_x + 4
    close = jnp.where(
        lane < width,
        result,
        jnp.where(lane < 2 * width, roll_lanes(result, width - 32), roll_lanes(result, 2 * (width - 32))),
    )
    half = out_ref.shape[1]
    share = jnp.where(lane_ids(half) < LANES // 2, close[:half], roll_lanes(close[WIN - half :], LANES // 2))
    for k in range(out_ref.shape[0]):
        out_ref[k] = share


WINDOW = pl.ds(TOP, WIN)
BEFORE = pl.ds(TOP - 1, WIN)
AFTER = pl.ds(TOP + 1, WIN)


def spot(x):
    if isinstance(x, int):
        return (0 if 0 <= x < 16 else 1), x % 16
    return 0, x


def beside(value, edge):
    lane = lane_ids(value.shape[0])
    down = jnp.where(lane == 0, edge, roll_lanes(value, 1))
    up = jnp.where(lane == LANES - 1, edge, roll_lanes(value, -1))
    return down, up


def from_edge(tile, g):
    return roll_lanes(tile, LANES - 4 - 8 * g)


def to_edge(old, plane, g):
    lane = lane_ids()
    here = (lane // 8 == g) & ((lane % 8 == 3) | (lane % 8 == 4))
    return jnp.where(here, roll_lanes(plane, 8 * g + 4), old)


def beside_edge(own_ref, other, middle):
    lane = lane_ids()
    place = lane % 8
    own = own_ref[WINDOW, :]
    left = jnp.where(lane >= 8, roll_lanes(own, 8), roll_lanes(other, 8))
    right = jnp.where(lane < LANES - 8, roll_lanes(own, -8), roll_lanes(other, -8))
    minus = jnp.where(place == 4, middle, roll_lanes(own, 1))
    plus = jnp.where(place == 3, middle, roll_lanes(own, -1))
    return left, right, own_ref[BEFORE, :], own_ref[AFTER, :], minus, plus


def normalised(own, others):
    faces = [0.5 * (own + other) for other in others]
    total = functools.reduce(lambda a, b: a + b, faces)
    inside = own > 0.0
    factor = jnp.where(inside, OMEGA / jnp.where(inside, total, 1.0), 0.0)
    return [face * factor for face in faces]


def relaxed(own, others, weights):
    new = (1.0 - OMEGA) * own
    for weight, other in zip(weights, others):
        new = new + weight * other
    return new


def zeros():
    return jnp.zeros((WIN, LANES), jnp.float32)


def wall_lane():
    return (lane_ids() == 0) & (lax.axis_index("gz") == 0)


def column_of(rbf, ch, x, cells_x):
    return roll_lanes(rbf, 2 * LANES - 2 - (cells_x + 4) * ch - x)


def inner_kernel(
    count_z, prev_ref, stiff_ref, edge_ref, yabove_ref, ybelow_ref, shares_ref,
    u0_ref, u1_ref, u2_ref, s_ref, w_ref, es_ref, cs_ref, c_ref, rbf_ref, widev_ref, done_ref,
    e_ref, ew_ref,
):
    _, cells_x, cells_y, cells_z = prev_ref.shape
    first = wall_lane()
    scale = wall_scale(count_z, cells_z)
    main = pl.ds(TOP + 2, cells_y)

    def assemble(ch, x):
        at = (ch * cells_x + x) * HALO
        plane = u0_ref.at[ch, x] if ch < 3 else s_ref.at[x]
        plane[main, :] = prev_ref[ch, x] if ch < 3 else stiff_ref[x] * scale
        plane[TOP - 1 : TOP + 2, :] = ybelow_ref[at : at + HALO, :]
        plane[TOP + 2 + cells_y : TOP + 2 + cells_y + HALO, :] = yabove_ref[at : at + HALO, :]

    for x in range(cells_x):
        assemble(3, x)
    for ch in range(4):
        fill(widev_ref.at[ch], ybelow_ref, edge_ref[ch], yabove_ref, (4 * cells_x + ch) * HALO)
    es_ref[WINDOW, :] = widev_ref[3]
    ends = zeros()
    for x in range(cells_x):
        ends = to_edge(ends, s_ref[x, WINDOW, :], x)
    cs_ref[...] = ends

    def weigh(x, carry):
        own = s_ref[x, WINDOW, :]
        down, up = beside(own, from_edge(es_ref[WINDOW, :], x))
        others = (s_ref[x - 1, WINDOW, :], s_ref[x + 1, WINDOW, :], s_ref[x, BEFORE, :], s_ref[x, AFTER, :], down, up)
        for k, weight in enumerate(normalised(own, others)):
            w_ref[k, x] = weight
        return carry

    for x in range(1, cells_x - 1):
        weigh(x, 0)
    others = beside_edge(es_ref, zeros(), cs_ref[...])
    for k, weight in enumerate(normalised(es_ref[WINDOW, :], others)):
        ew_ref[k] = weight

    for ch in range(3):
        e_ref[0, ch, WINDOW, :] = widev_ref[ch]
        for x in range(cells_x):
            assemble(ch, x)
    rbf_ref[...] = zeros()

    @pl.when(lax.axis_index("gz") == 0)
    def _():
        share = shares_ref[0]
        for k in range(1, shares_ref.shape[0]):
            share = share + shares_ref[k]
        half = share.shape[0]
        rbf_ref[WIN - half :, :] = roll_lanes(share, LANES // 2)
        rbf_ref[:half, :] = share
        rbf = rbf_ref[...]

        def layer(x, carry):
            own = first & (s_ref[x, WINDOW, :] > 0.0)
            for ch in range(3):
                column = column_of(rbf, ch, x, cells_x)
                u0_ref[ch, x, WINDOW, :] = jnp.where(own, column, u0_ref[ch, x, WINDOW, :])
            return carry

        for x in range(cells_x):
            layer(x, 0)

    stages = (u0_ref, u1_ref, u2_ref)
    for sweep in range(SWEEPS):
        now, last = stages[sweep], sweep == SWEEPS - 1

        rows, weigh_rows, above, below, held = (
            (pl.ds(TOP + 2, cells_y), pl.ds(2, cells_y), pl.ds(TOP + 1, cells_y), pl.ds(TOP + 3, cells_y), first[:cells_y])
            if last
            else (WINDOW, pl.ds(0, WIN), BEFORE, AFTER, first)
        )
        for x in range(1 + sweep, cells_x - 1 - sweep):
            weights = [w_ref[k, x, weigh_rows, :] for k in range(6)]
            for ch in range(3):
                own = now[ch, x, rows, :]
                down, up = beside(own, from_edge(e_ref[sweep, ch, rows, :], x))
                others = (
                    now[ch, x - 1, rows, :],
                    now[ch, x + 1, rows, :],
                    now[ch, x, above, :],
                    now[ch, x, below, :],
                    down,
                    up,
                )
                new = jnp.where(held, own, relaxed(own, others, weights))
                if last:
                    done_ref[ch, x] = new
                else:
                    stages[sweep + 1][ch, x, WINDOW, :] = new
        if not last:
            for ch in range(3):
                ends = zeros()
                for x in range(sweep, cells_x - sweep):
                    ends = to_edge(ends, now[ch, x, WINDOW, :], x)
                c_ref[sweep, ch] = ends
                others = beside_edge(e_ref.at[sweep, ch], zeros(), ends)
                weights = [ew_ref[k] for k in range(6)]
                e_ref[sweep + 1, ch, WINDOW, :] = relaxed(e_ref[sweep, ch, WINDOW, :], others, weights)


def outer_kernel(
    u0_ref, u1_ref, u2_ref, s_ref, w_ref, wide_ref, es_ref, cs_ref, c_ref, rbf_ref, done_ref, xabove_ref, xbelow_ref,
    out_ref,
    h0_ref, h1_ref, h2_ref, hs_ref, hw_ref, e_ref, eside_ref, ew_ref, new_ref, sems,
):
    _, cells_x, _, _ = u0_ref.shape
    cells_y = done_ref.shape[2]
    lane = lane_ids()
    first = wall_lane()
    inside = pl.ds(HALO, cells_x - 2 * HALO)
    copies = [pltpu.make_async_copy(done_ref.at[ch, inside], out_ref.at[ch, inside], sems.at[ch]) for ch in range(3)]
    for copy in copies:
        copy.start()

    def held(x):
        return x + HALO if x < HALO else x - cells_x + HALO + 6

    beyond = [x for p in range(HALO) for x in (p - HALO, cells_x + p)]
    for x in beyond:
        source, p = (xbelow_ref, x + HALO) if x < 0 else (xabove_ref, x - cells_x)
        own = source[3 * HALO + p]
        hs_ref[held(x), WINDOW, :] = own
        for ch in range(3):
            column = column_of(rbf_ref[...], ch, x, cells_x)
            h0_ref[ch, held(x), WINDOW, :] = jnp.where(first & (own > 0.0), column, source[ch * HALO + p])
    for ch in range(4):
        above = roll_lanes(xabove_ref[4 * HALO], -32 * ch)
        below = roll_lanes(xbelow_ref[4 * HALO], -32 * ch)
        side = jnp.where(lane < 8 * HALO, above, jnp.where(lane >= LANES - 8 * HALO, below, 0.0))
        if ch < 3:
            e_ref[0, ch, 0, WINDOW, :] = wide_ref[ch]
            e_ref[0, ch, 1, WINDOW, :] = side
        else:
            eside_ref[WINDOW, :] = side

    def stiff(x):
        return s_ref.at[x] if 0 <= x < cells_x else hs_ref.at[held(x)]

    def field(sweep, ch, x):
        if sweep <= x < cells_x - sweep:
            return (u0_ref, u1_ref, u2_ref)[sweep].at[ch, x]
        return (h0_ref, h1_ref, h2_ref)[sweep].at[ch, held(x)]

    edge_stiff = (es_ref, eside_ref)

    ends = zeros()
    for x in (-1, cells_x):
        ends = to_edge(ends, stiff(x)[WINDOW, :], spot(x)[1])
    for tile, middle in ((0, cs_ref[...]), (1, ends)):
        others = beside_edge(edge_stiff[tile], edge_stiff[1 - tile][WINDOW, :], middle)
        for k, weight in enumerate(normalised(edge_stiff[tile][WINDOW, :], others)):
            ew_ref[k, tile] = weight
    for x in (-2, -1, 0, cells_x - 1, cells_x, cells_x + 1):
        own = stiff(x)[WINDOW, :]
        tile, g = spot(x)
        down, up = beside(own, from_edge(edge_stiff[tile][WINDOW, :], g))
        others = (
            stiff(x - 1)[WINDOW, :],
            stiff(x + 1)[WINDOW, :],
            stiff(x)[BEFORE, :],
            stiff(x)[AFTER, :],
            down,
            up,
        )
        for k, weight in enumerate(normalised(own, others)):
            hw_ref[k, held(x)] = weight

    for sweep in range(SWEEPS):
        last = sweep == SWEEPS - 1
        rows, weigh_rows, above, below, fixed = (
            (pl.ds(TOP + 2, cells_y), pl.ds(2, cells_y), pl.ds(TOP + 1, cells_y), pl.ds(TOP + 3, cells_y), first[:cells_y])
            if last
            else (WINDOW, pl.ds(0, WIN), BEFORE, AFTER, first)
        )
        planes = [x for p in range(HALO) for x in (sweep - 2 + p, cells_x + 1 - sweep - p)]
        for x in planes:
            tile, g = spot(x)
            if 1 <= x < cells_x - 1:
                weights = [w_ref[k, x, weigh_rows, :] for k in range(6)]
            else:
                weights = [hw_ref[k, held(x), weigh_rows, :] for k in range(6)]
            for ch in range(3):
                here = field(sweep, ch, x)
                own = here[rows, :]
                down, up = beside(own, from_edge(e_ref[sweep, ch, tile, rows, :], g))
                others = (
                    field(sweep, ch, x - 1)[rows, :],
                    field(sweep, ch, x + 1)[rows, :],
                    here[above, :],
                    here[below, :],
                    down,
                    up,
                )
                new = jnp.where(fixed, own, relaxed(own, others, weights))
                if last:
                    place = x if x < HALO else x - cells_x + 2 * HALO
                    new_ref[ch, place] = new
                    sem = sems.at[3 + 6 * ch + place]
                    copies.append(pltpu.make_async_copy(new_ref.at[ch, place], out_ref.at[ch, x], sem))
                    copies[-1].start()
                else:
                    (h1_ref, h2_ref)[sweep][ch, held(x), WINDOW, :] = new
        if last:
            break
        for ch in range(3):
            if sweep == 0:
                ends = zeros()
                for x in (-1, cells_x):
                    ends = to_edge(ends, field(0, ch, x)[WINDOW, :], spot(x)[1])
                middles = (c_ref[0, ch], ends)
            else:
                ends = c_ref[1, ch]
                for x in (0, cells_x - 1):
                    ends = to_edge(ends, field(1, ch, x)[WINDOW, :], x)
                middles = (ends,)
            for tile, middle in enumerate(middles):
                others = beside_edge(e_ref.at[sweep, ch, tile], e_ref[sweep, ch, 1 - tile, WINDOW, :], middle)
                weights = [ew_ref[k, tile] for k in range(6)]
                e_ref[sweep + 1, ch, tile, WINDOW, :] = relaxed(
                    e_ref[sweep, ch, tile, WINDOW, :], others, weights
                )
    for copy in copies:
        copy.wait()


def step(value, axis, by):
    size = lax.axis_size(axis)
    return lax.ppermute(value, axis, [(i, i + by) for i in range(size) if 0 <= i + by < size])


def body(centre_coef, centre_index, stiff_factor, prev_disp):
    cells_x, cells_y, cells_z = stiff_factor.shape
    count_x = cells_x * lax.axis_size("gx")
    count_y = cells_y * lax.axis_size("gy")
    count_z = cells_z * lax.axis_size("gz")
    blocks = lax.axis_size("gx") * lax.axis_size("gy")
    depth = lax.axis_size("gz")
    scratch = pltpu.VMEM
    num = jnp.float32

    rows_y = 4 * cells_x * HALO
    row, low, high, ylow, yhigh = kernel_call(
        functools.partial(begin_kernel, float(count_z)),
        "pack_z",
        (
            f32(8, LANES),
            f32(2, cells_y, LANES),
            f32(2, cells_y, LANES),
            f32(rows_y, LANES),
            f32(rows_y, LANES),
        ),
        2000 * MEGA,
        (),
        (
            scratch((3, cells_x, cells_y, LANES), num),
            scratch((cells_x, cells_y, LANES), num),
            scratch((4, cells_y, LANES), num),
            scratch((3, centre_index.shape[0]), num),
            scratch((1, centre_index.shape[0]), jnp.int32),
            pltpu.SemaphoreType.DMA((6,)),
        ),
        far=tuple(in_hbm(a) for a in (prev_disp, stiff_factor, centre_coef.T, centre_index[None])),
    )
    zabove, zbelow = step(low, "gz", -1), step(high, "gz", 1)

    along_x, along_y = lax.axis_size("gx"), lax.axis_size("gy")
    other = lax.ppermute(row, "gx", [(i, i ^ 1) for i in range(along_x)])
    (rows,) = kernel_call(pair_kernel, "pair", (f32(blocks, LANES),), 500 * MEGA, (row, other))
    every_second = [[x * along_y + y for x in range(k, along_x, 2) for y in range(along_y)] for k in range(2)]
    centres = lax.all_to_all(
        rows.reshape(blocks // 2, 2, LANES), ("gx", "gy"), 0, 0, tiled=True, axis_index_groups=every_second
    )

    rows_all = -(-(rows_y + 4 * HALO) // 8) * 8
    edge, ylow, yhigh = kernel_call(
        pack_y_kernel,
        "pack_y",
        (f32(4, cells_y, LANES), f32(rows_all, LANES), f32(rows_all, LANES)),
        300 * MEGA,
        (zabove, zbelow, ylow, yhigh),
    )
    yabove, ybelow = step(ylow, "gy", -1), step(yhigh, "gy", 1)

    table = stencil(count_x, count_y, count_z)
    (share,) = kernel_call(
        functools.partial(rbf_kernel, table, cells_x, cells_y, count_y),
        "rbf",
        (f32(depth, HALF, LANES),),
        1500 * MEGA,
        (centres.reshape(blocks, LANES),),
        (scratch((ROWS, LANES), num),),
        after=(ylow,),
    )
    shares = lax.all_to_all(share, "gz", 0, 0, tiled=True)

    xlow, xhigh = kernel_call(
        functools.partial(pack_x_kernel, float(count_z)),
        "pack_x",
        (far_out(4 * HALO + 1, WIN, LANES), far_out(4 * HALO + 1, WIN, LANES)),
        8000 * MEGA,
        (edge, yabove, ybelow, prev_disp, stiff_factor),
        (scratch((4, WIN, LANES), num),),
    )
    xabove, xbelow = step(xlow, "gx", -1), step(xhigh, "gx", 1)

    u0, u1, u2, s, w, es, cs, c, rbf, wide, done = kernel_call(
        functools.partial(inner_kernel, float(count_z)),
        "inner",
        (
            near(3, cells_x, ROWS, LANES),
            near(3, cells_x, ROWS, LANES),
            near(3, cells_x, ROWS, LANES),
            near(cells_x, ROWS, LANES),
            near(6, cells_x, WIN, LANES),
            near(ROWS, LANES),
            near(WIN, LANES),
            near(2, 3, WIN, LANES),
            near(WIN, LANES),
            near(4, WIN, LANES),
            near(3, cells_x, cells_y, cells_z),
        ),
        9000 * MEGA,
        (prev_disp, stiff_factor, in_hbm(edge), yabove, ybelow, shares),
        (
            scratch((3, 3, ROWS, LANES), num),
            scratch((6, WIN, LANES), num),
        ),
    )

    (out,) = kernel_call(
        outer_kernel,
        "outer",
        (Far((3, cells_x, cells_y, cells_z), num),),
        5500 * MEGA,
        (u0, u1, u2, s, w, wide, es, cs, c, rbf, done, xabove, xbelow),
        (
            scratch((3, 12, ROWS, LANES), num),
            scratch((3, 12, ROWS, LANES), num),
            scratch((3, 12, ROWS, LANES), num),
            scratch((12, ROWS, LANES), num),
            scratch((6, 12, WIN, LANES), num),
            scratch((3, 3, 2, ROWS, LANES), num),
            scratch((ROWS, LANES), num),
            scratch((6, 2, WIN, LANES), num),
            scratch((3, 2 * HALO, cells_y, LANES), num),
            pltpu.SemaphoreType.DMA((21,)),
        ),
    )
    return out


def solution(mesh):
    placed = (
        P(("gx", "gy", "gz"), None),
        P(("gx", "gy", "gz")),
        P("gx", "gy", "gz"),
        P(None, "gx", "gy", "gz"),
    )
    return jax.shard_map(
        body, mesh=mesh, in_specs=placed, out_specs=P(None, "gx", "gy", "gz"), check_vma=False
    )
```
